256 devices in a mesh: replica: 2 (over core), lists: 128 (over z, x, y).
Axes of the slice: x: 4, y: 4, z: 8, core: 2. Of those that a mesh axis runs over, the one named last changes fastest.
Arguments:
- inserts: bfloat16 [32768, 1024], P(('replica', 'lists')), may hold values from -6 to 6
- list_ids: int32 [32768], P(('replica', 'lists')), may hold values from 0 to 131071, as said below
- centroids: bfloat16 [131072, 1024], P('lists'), may hold values from -6 to 6
- prior_counts: int32 [131072], P('lists'), may hold values from 1 to 16
- rotation: bfloat16 [1024, 1024], replicated, may hold values from -0.1875 to 0.1875
Outputs:
- new_centroids: bfloat16 [131072, 1024], P('lists')
- rotated: bfloat16 [32768, 1024], P(('replica', 'lists'))
The draws below stay inside these ranges and needn't reach their ends.
Inputs may be any that keep to these rules, and one draw needn't show every extreme that they name: `list_ids`: list k belongs to index k // 1024 of lists. In each aligned block of 128 inserts (the rows of one device) at most 4 inserts name lists of one index; in every draw one index receives exactly 4 from every block, every other index at most 1.
All inputs are finite; a program needn't handle non-finite values.
Results may differ from the reference program's by a relative error of at most 0.0055.
Values may be sent and summed in bfloat16 or wider, within the bound.
A program may use at most 128 MiB of HBM per device.

```python
import jax
import jax.numpy as jnp

D = 1024
LISTS_DEV = 1024
ROWS_DEV = 128
LISTS = 131072
INSERTS = 32768
SLOT = 4


def draw_list_ids(key, part):
    owners = LISTS // LISTS_DEV
    blocks = INSERTS // ROWS_DEV
    key_hot, key_shuffle, key_first, key_second = jax.random.split(key, 4)
    hot_owner = jax.random.randint(key_hot, (), 0, owners)
    position_in = jnp.arange(ROWS_DEV, dtype=jnp.int32)
    spread_owner = (hot_owner + 1 + (position_in - SLOT) % (owners - 1)) % owners
    owner_row = jnp.where(position_in < SLOT, hot_owner, spread_owner)
    shuffles = jax.vmap(lambda single: jax.random.permutation(single, ROWS_DEV))(jax.random.split(key_shuffle, blocks))
    owner_of = owner_row[shuffles]
    first_draw = jax.random.randint(key_first, (blocks, ROWS_DEV), 0, LISTS_DEV)
    second_draw = jax.random.randint(key_second, (blocks, ROWS_DEV), 0, LISTS_DEV)
    within_owner = first_draw * second_draw // LISTS_DEV
    return (owner_of * LISTS_DEV + within_owner).reshape(-1).astype(jnp.int32)


def plant(entries, rng, low, top_value):
    longest = entries.shape.index(max(entries.shape))
    spots = []
    for shift in (0, 1):
        where = [jax.random.randint(jax.random.fold_in(rng, axis), (), 0, length) for axis, length in enumerate(entries.shape)]
        where[longest] = (where[longest] + shift) % entries.shape[longest]
        spots.append(tuple(where))
    return entries.at[spots[0]].set(low).at[spots[1]].set(top_value)


def steps_of(rng, extent, cuts, low, top_value):
    gain = 1.0
    for position, shards_of in cuts:
        heights = jax.random.uniform(jax.random.fold_in(jax.random.fold_in(rng, 6), position), (shards_of,), jnp.float32, low / len(cuts), top_value / len(cuts))
        gain = gain * jnp.repeat(jnp.exp(heights), extent[position] // shards_of).reshape((-1,) + (1,) * (len(extent) - 1 - position))
    return gain


def noise(stream_key, dims, spread, bound, pieces=(), held_as=jnp.bfloat16):
    values = jax.random.normal(stream_key, dims, jnp.float32) * spread
    if len(pieces) > 0:
        values = steps_of(stream_key, dims, pieces, -0.22, 0.18) * values
    return jnp.clip(values, min=-bound, max=bound).astype(held_as)


def setup_inputs(seed: int = 0) -> dict:
    key_of = jax.random.split(jax.random.key(seed), 6)
    inserts = noise(key_of[0], (INSERTS, D), 1.0, 6.0, ((0, 256),))
    list_ids = draw_list_ids(jax.random.fold_in(key_of[5], 71), 0)
    centroids = noise(key_of[2], (LISTS, D), 1.0, 6.0, ((0, 128),))
    prior_counts = plant(jax.random.randint(key_of[3], (LISTS,), 1, 17), jax.random.fold_in(key_of[3], 1), 1, 16).astype(jnp.int32)
    rotation = noise(key_of[4], (D, D), D ** -0.5, 0.1875)
    return {"inserts": inserts, "list_ids": list_ids, "centroids": centroids, "prior_counts": prior_counts, "rotation": rotation}


def reference(inserts, list_ids, centroids, prior_counts, rotation):
    values = inserts.astype(jnp.float32)
    sums = jax.ops.segment_sum(values, list_ids, num_segments=LISTS)
    counts = jax.ops.segment_sum(jnp.ones((INSERTS,), jnp.float32), list_ids, num_segments=LISTS)
    old_float = centroids.astype(jnp.float32)
    denominator = prior_counts.astype(jnp.float32) + counts
    updated = old_float + (sums - counts[:, None] * old_float) / denominator[:, None]
    new_centroids = updated.astype(jnp.bfloat16)
    picked = new_centroids[list_ids].astype(jnp.float32)
    residual_rows = (values - picked).astype(jnp.bfloat16)
    rotated = jnp.dot(residual_rows, rotation, preferred_element_type=jnp.float32).astype(jnp.bfloat16)
    return new_centroids, rotated
```

```python
import jax
import jax.numpy as jnp
from jax import lax
from jax.experimental import pallas as pl
from jax.experimental.pallas import tpu as pltpu
from jax.sharding import PartitionSpec as P

MESH = pl.DeviceIdType.MESH
BF = jnp.bfloat16
F32 = jnp.float32
I32 = jnp.int32
STAGES = 20


def mm(a, b):
    return jnp.dot(a, b, preferred_element_type=F32)


def iota(shape, dim):
    return lax.broadcasted_iota(I32, shape, dim)


def onehot(mask):
    return jnp.where(mask, 1.0, 0.0).astype(BF)


def owner_at(zz, gg):
    return (zz << 4) + ((gg & 3) << 2) + (gg >> 2)


def wait_bytes(ref, sem):
    pltpu.make_async_copy(ref, ref, sem).wait()


def kernel(
    ids_ref, x_ref, prior_ref, cent_hbm, rot_hbm, newc_hbm, out_ref,
    sbuf, r1, bbuf, rb1, a2, ra2, b2, rb2, hot_a, hot_b, idb,
    w, wt, cnt, rinv, cvm, rvm, nvm, rowsb,
    ga, gb, gha, ghb, rga, rgb, rha, rhb, fa, fb, rfa, rfb,
    h2a, h2b, rh2a, rh2b, ht, rht, perm, send, recv, local,
):
    c = lax.axis_index("replica")
    li = lax.axis_index("lists")
    z = li // 16
    x = (li // 4) % 4
    y = li % 4
    zc = z * 2 + c
    g = y * 4 + x

    def dev(zc_to, g_to):
        return (zc_to % 2, (zc_to // 2) * 16 + (g_to % 4) * 4 + g_to // 4)

    def start(stage, src, dst, zc_to, g_to):
        pltpu.make_async_remote_copy(
            src_ref=src, dst_ref=dst, send_sem=send.at[stage], recv_sem=recv.at[stage],
            device_id=dev(zc_to, g_to), device_id_type=MESH,
        ).start()

    def along_zc(stage, src, dst):
        @pl.loop(1, 16)
        def _(step):
            to = (zc + step) % 16
            start(stage, src.at[to], dst.at[zc], to, g)

    def along_g(stage, src, dst):
        @pl.loop(1, 16)
        def _(step):
            to = (g + step) % 16
            start(stage, src.at[to], dst.at[g], zc, to)

    barrier = pltpu.get_barrier_semaphore()

    @pl.loop(1, 16)
    def _(step):
        pl.semaphore_signal(barrier, 1, device_id=dev((zc + step) % 16, g), device_id_type=MESH)
        pl.semaphore_signal(barrier, 1, device_id=dev(zc, (g + step) % 16), device_id_type=MESH)

    half = pl.ds(pl.multiple_of(c * 512, 512), 512)
    cent_copy = pltpu.make_async_copy(cent_hbm.at[:, half], cvm, local.at[0])
    rot_copy = pltpu.make_async_copy(rot_hbm, rvm, local.at[1])
    cent_copy.start()
    rot_copy.start()

    ids = ids_ref[...]
    owner_row = ids >> 10
    eye = iota((128, 128), 0) == iota((128, 128), 1)
    owner_col = jnp.sum(jnp.where(eye, owner_row, 0), axis=1, keepdims=True)
    same = jnp.where(owner_col == owner_row, 1.0, 0.0)
    earlier = jnp.where(iota((128, 128), 0) < iota((128, 128), 1), same, 0.0)
    later = jnp.where(iota((128, 128), 1) < iota((128, 128), 0), same, 0.0)
    hot_row = jnp.sum(same, axis=0, keepdims=True) > 1.5
    hot_col = jnp.sum(same, axis=1, keepdims=True) > 1.5
    slot_row = jnp.where(hot_row, jnp.sum(earlier, axis=0, keepdims=True), 4.0)
    slot_col = jnp.where(hot_col, jnp.sum(later, axis=1, keepdims=True), 4.0)

    r128 = iota((128, 128), 0)
    cold_owner_row = jnp.where(hot_row, -1, owner_row)
    pick = onehot(owner_at(r128 >> 4, r128 & 15) == cold_owner_row)
    for cc in range(2):
        block = mm(pick, x_ref[:, cc * 512 : cc * 512 + 256]).astype(BF)
        for t in range(2):
            sbuf[:, cc, t * 16 : t * 16 + 16, :] = block[:, t * 128 : t * 128 + 128].reshape(8, 16, 128)
    tile_row = iota((16, 128), 0)
    for cc in range(2):
        tile = jnp.zeros((16, 128), F32)
        for j in range(4):
            match = (tile_row >> 2 == j) & ((tile_row & 3).astype(F32) == slot_row)
            low = cc * 512 + j * 128
            tile = tile + mm(onehot(match), x_ref[:, low : low + 128])
        sbuf[:, cc, 32:48, :] = jnp.broadcast_to(tile.astype(BF)[None], (8, 16, 128))
    info = jnp.where(tile_row == 0, owner_row, 0)
    info = jnp.where(tile_row == 1, (ids & 1023) >> 5, info)
    info = jnp.where(tile_row == 2, ids & 31, info).astype(F32)
    info = jnp.where(tile_row == 3, slot_row, info).astype(BF)
    for cc in range(2):
        sbuf[:, cc, 48:64, :] = jnp.broadcast_to(info[None], (8, 16, 128))

    r256 = iota((256, 128), 0)
    hit = owner_at((r256 & 15) >> 1, r256 >> 4) == cold_owner_row
    part_b = mm(onehot(hit & ((r256 & 1) == 0)), x_ref[:, 256:512])
    part_b = part_b + mm(onehot(hit & ((r256 & 1) == 1)), x_ref[:, 768:1024])
    bbuf[...] = part_b.astype(BF).reshape(16, 16, 256)

    p0, p1 = iota((256, 256), 0), iota((256, 256), 1)
    perm[...] = onehot((p0 >> 4 == p1 & 15) & (p0 & 15 == p1 >> 4))

    def swap(rows):
        return mm(perm[...], rows).astype(BF)

    sflat = sbuf.at[z, c]
    r1[zc] = sflat[...]
    rb1[g] = bbuf[g]
    pl.semaphore_wait(barrier, 30)

    @pl.loop(1, 16)
    def _(step):
        to = (zc + step) % 16
        start(0, sbuf.at[to // 2, to % 2], r1.at[zc], to, g)

    along_g(1, bbuf, rb1)

    ones = jnp.ones((128, 128), BF)
    for a in range(8):
        diag = jnp.where(eye, prior_ref[a : a + 1, :].astype(F32), 0.0).astype(BF)
        rinv[a * 128 : a * 128 + 128, :] = mm(diag, ones)

    wait_bytes(r1.at[pl.ds(0, 15)], recv.at[0])
    hot = swap(r1[:, 32:48, :].reshape(256, 128)).reshape(4, 4, 16, 128)
    hot_a[:, y, x, :, 0:128] = hot[0]
    hot_a[:, y, x, :, 128:256] = hot[1]
    hot_b[:, y, x, :, 0:128] = hot[2]
    hot_b[:, y, x, :, 128:256] = hot[3]
    got = mm(perm[...], r1[:, 48:64, :].reshape(256, 128)).astype(I32)
    idb[y, x] = (got[48:64] << 17) + (got[0:16] << 10) + (got[16:32] << 5) + got[32:48]
    for step in range(1, 4):
        to = y * 4 + (x + step) % 4
        start(4, hot_a.at[:, y, x], hot_a.at[:, y, x], zc, to)
        start(8, idb.at[y, x], idb.at[y, x], zc, to)
        start(6, hot_b.at[:, y, x], hot_b.at[:, y, x], zc, ((y + step) % 4) * 4 + x)
    for t in range(2):
        moved = swap(r1[:, t * 16 : t * 16 + 16, :].reshape(256, 128))
        a2[:, :, t * 128 : t * 128 + 128] = moved.reshape(16, 16, 128)
    ra2[g] = a2[g]
    along_g(2, a2, ra2)

    wait_bytes(rb1.at[pl.ds(0, 15)], recv.at[1])
    b2[...] = swap(rb1[...].reshape(256, 256)).reshape(16, 16, 256)
    rb2[zc] = b2[zc]
    along_zc(3, b2, rb2)

    wait_bytes(hot_a.at[:, 0, pl.ds(0, 3)], recv.at[4])
    wait_bytes(idb.at[0, pl.ds(0, 3)], recv.at[8])
    wait_bytes(hot_b.at[:, 0, pl.ds(0, 3)], recv.at[6])
    for step in range(1, 4):
        to = ((y + step) % 4) * 4 + x
        start(9, idb.at[y], idb.at[y], zc, to)
        start(5, hot_a.at[:, y], hot_a.at[:, y], zc, to)
        start(7, hot_b.at[:, :, x], hot_b.at[:, :, x], zc, y * 4 + (x + step) % 4)

    wait_bytes(idb.at[pl.ds(0, 3)], recv.at[9])
    code = idb[...].reshape(256, 128)
    mine = ((code >> 10) & 127) == li
    slot = code >> 17
    number = (code & 1023) + 1
    ones8 = jnp.ones((8, 256), BF)
    ones256 = jnp.ones((256, 128), BF)
    for block, s in enumerate((4, 0, 1, 2, 3)):
        here = mine & (slot == s)
        top = jnp.where(here, number & 2016, 0).astype(F32).astype(BF)
        low = jnp.where(here, number & 31, 0).astype(F32).astype(BF)
        both = jnp.concatenate([top, low], axis=1)
        lanes = lax.dot_general(ones8, both, (((1,), (1,)), ((), ())), preferred_element_type=F32)
        lanes = lanes.astype(I32)[0:1, :] - 1
        rows = mm(both, ones256).astype(I32) - 1
        for a in range(8):
            w[a * 128 : a * 128 + 128, block * 256 : block * 256 + 256] = onehot(
                iota((128, 256), 0) + a * 128 == lanes
            )
            wt[block * 256 : block * 256 + 256, a * 128 : a * 128 + 128] = onehot(
                iota((256, 128), 1) + a * 128 == rows
            )
    for a in range(4):
        lists = slice(a * 256, a * 256 + 256)
        total = mm(w[lists, :], jnp.ones((1280, 128), BF))
        cnt[lists, :] = total
        rinv[lists, :] = 1.0 / (rinv[lists, :] + total)

    def refresh(part, cold, hot_rows):
        for a in range(4):
            lists = slice(a * 256, a * 256 + 256)
            cols = slice(part * 256, part * 256 + 256)
            sums = mm(w[lists, 0:256], cold) + mm(w[lists, 256:1280], hot_rows)
            old = cvm[lists, cols].astype(F32)
            count = jnp.concatenate([cnt[lists, :]] * 2, axis=1)
            scale = jnp.concatenate([rinv[lists, :]] * 2, axis=1)
            nvm[lists, cols] = (old + (sums - count * old) * scale).astype(BF)
        return nvm[:, part * 256 : part * 256 + 256]

    cent_copy.wait()
    wait_bytes(ra2.at[pl.ds(0, 15)], recv.at[2])
    wait_bytes(hot_a.at[:, pl.ds(0, 3)], recv.at[5])
    new_a = refresh(0, ra2[...].reshape(256, 256), hot_a[...].reshape(1024, 256))
    gha[...] = mm(wt[256:1280, :], new_a).astype(BF).reshape(4, 4, 4, 16, 256)
    for step in range(1, 4):
        to = (y + step) % 4
        start(12, gha.at[:, to], rha.at[y], zc, to * 4 + x)
    ga[...] = mm(wt[0:256, :], new_a).astype(BF).reshape(16, 16, 256)
    rga[g] = ga[g]
    along_g(10, ga, rga)
    rha[y] = gha[:, y]

    wait_bytes(rb2.at[pl.ds(0, 15)], recv.at[3])
    wait_bytes(hot_b.at[:, :, pl.ds(0, 3)], recv.at[7])
    rowsb[...] = swap(rb2[...].reshape(256, 256))
    new_b = refresh(1, rowsb[...], hot_b[...].reshape(1024, 256))
    ghb[...] = mm(wt[256:1280, :], new_b).astype(BF).reshape(4, 4, 4, 16, 256)
    for step in range(1, 4):
        to = (x + step) % 4
        start(13, ghb.at[:, :, to], rhb.at[x], zc, y * 4 + to)
    gb[...] = swap(mm(wt[0:256, :], new_b).astype(BF)).reshape(16, 16, 256)
    rgb[zc] = gb[zc]
    along_zc(11, gb, rgb)
    rhb[x] = ghb[:, :, x]

    start(19, nvm, newc_hbm.at[:, half], zc + 1 - 2 * c, g)
    own_copy = pltpu.make_async_copy(nvm, newc_hbm.at[:, half], local.at[2])
    own_copy.start()

    wait_bytes(rga.at[pl.ds(0, 15)], recv.at[10])
    fa[...] = swap(rga[...].reshape(256, 256)).reshape(16, 16, 256)
    rfa[zc] = fa[zc]
    along_zc(14, fa, rfa)

    wait_bytes(rgb.at[pl.ds(0, 15)], recv.at[11])
    fb[...] = swap(rgb[...].reshape(256, 256)).reshape(16, 16, 256)
    rfb[g] = fb[g]
    along_g(15, fb, rfb)

    wait_bytes(rha.at[pl.ds(0, 3)], recv.at[12])
    h2a[...] = (rha[0] + rha[1]) + (rha[2] + rha[3])
    for step in range(1, 4):
        to = (x + step) % 4
        start(16, h2a.at[:, to], rh2a.at[x], zc, y * 4 + to)
    rh2a[x] = h2a[:, x]
    wait_bytes(rhb.at[pl.ds(0, 3)], recv.at[13])
    h2b[...] = (rhb[0] + rhb[1]) + (rhb[2] + rhb[3])
    for step in range(1, 4):
        to = (y + step) % 4
        start(17, h2b.at[:, to], rh2b.at[y], zc, to * 4 + x)
    rh2b[y] = h2b[:, y]

    wait_bytes(rh2a.at[pl.ds(0, 3)], recv.at[16])
    wait_bytes(rh2b.at[pl.ds(0, 3)], recv.at[17])
    back_a = ((rh2a[0] + rh2a[1]) + (rh2a[2] + rh2a[3])).reshape(64, 256)
    back_b = ((rh2b[0] + rh2b[1]) + (rh2b[2] + rh2b[3])).reshape(64, 256)
    back = jnp.concatenate([back_a[:, :128], back_a[:, 128:], back_b[:, :128], back_b[:, 128:]], axis=0)
    ht[...] = swap(back).reshape(16, 16, 128)
    rht[zc] = ht[zc]
    along_zc(18, ht, rht)

    lane = iota((128, 256), 1)
    cold_owner_col = jnp.where(hot_col, -1, owner_col)
    hit_a = owner_at(lane >> 5, lane & 15) == cold_owner_col
    hit_b = owner_at((lane & 15) >> 1, lane >> 4) == cold_owner_col
    wait_bytes(rfa.at[pl.ds(0, 15)], recv.at[14])
    wait_bytes(rfb.at[pl.ds(0, 15)], recv.at[15])
    picked = []
    for cc in range(2):
        picked.append(mm(onehot(hit_a & ((lane >> 4) & 1 == cc)), rfa[...].reshape(256, 256)))
        picked.append(mm(onehot(hit_b & (lane & 1 == cc)), rfb[...].reshape(256, 256)))
    wait_bytes(rht.at[pl.ds(0, 15)], recv.at[18])
    tile_lane = iota((128, 16), 1)
    tiles = []
    for cc in range(2):
        tile = rht[cc]
        for zz in range(1, 8):
            tile = tile + rht[zz * 2 + cc]
        for j in range(4):
            match = (tile_lane >> 2 == j) & ((tile_lane & 3).astype(F32) == slot_col)
            tiles.append(mm(onehot(match), tile))
    near = jnp.concatenate(picked, axis=1) + jnp.concatenate(tiles, axis=1)
    residual = (x_ref[...].astype(F32) - near).astype(BF)
    rot_copy.wait()
    for a in range(4):
        cols = slice(a * 256, a * 256 + 256)
        out_ref[:, cols] = mm(residual, rvm[:, cols]).astype(BF)

    own_copy.wait()
    wait_bytes(newc_hbm.at[:, half], recv.at[19])
    wait_bytes(sbuf.at[pl.ds(0, 7)], send.at[0])
    wait_bytes(sbuf.at[0, 0], send.at[0])
    for stage, ref in ((1, bbuf), (2, a2), (3, b2), (10, ga), (11, gb), (14, fa), (15, fb), (18, ht)):
        wait_bytes(ref.at[pl.ds(0, 15)], send.at[stage])
    wait_bytes(hot_a.at[:, 0, pl.ds(0, 3)], send.at[4])
    wait_bytes(hot_b.at[:, 0, pl.ds(0, 3)], send.at[6])
    wait_bytes(idb.at[0, pl.ds(0, 3)], send.at[8])
    wait_bytes(hot_a.at[:, pl.ds(0, 3)], send.at[5])
    wait_bytes(hot_b.at[:, :, pl.ds(0, 3)], send.at[7])
    wait_bytes(idb.at[pl.ds(0, 3)], send.at[9])
    wait_bytes(gha.at[:, pl.ds(0, 3)], send.at[12])
    wait_bytes(ghb.at[:, :, pl.ds(0, 3)], send.at[13])
    wait_bytes(h2a.at[:, pl.ds(0, 3)], send.at[16])
    wait_bytes(h2b.at[:, pl.ds(0, 3)], send.at[17])
    wait_bytes(nvm, send.at[19])


def per_device(inserts, list_ids, centroids, prior_counts, rotation):
    blocks = [
        pltpu.VMEM(shape, BF)
        for shape in (
            (8, 2, 64, 128), (16, 64, 128), (16, 16, 256), (16, 16, 256), (16, 16, 256), (16, 16, 256),
            (16, 16, 256), (16, 16, 256), (4, 4, 4, 16, 256), (4, 4, 4, 16, 256),
        )
    ]
    work = [
        pltpu.VMEM((4, 4, 16, 128), I32),
        pltpu.VMEM((1024, 1280), BF),
        pltpu.VMEM((1280, 1024), BF),
        pltpu.VMEM((1024, 128), F32),
        pltpu.VMEM((1024, 128), F32),
        pltpu.VMEM((1024, 512), BF),
        pltpu.VMEM((1024, 1024), BF),
        pltpu.VMEM((1024, 512), BF),
        pltpu.VMEM((256, 256), BF),
    ]
    back = [
        pltpu.VMEM(shape, BF)
        for shape in (
            (16, 16, 256), (16, 16, 256), (4, 4, 4, 16, 256), (4, 4, 4, 16, 256), (16, 16, 256), (16, 16, 256),
            (4, 4, 4, 16, 256), (4, 4, 4, 16, 256), (16, 16, 256), (16, 16, 256), (16, 16, 256), (16, 16, 256),
            (4, 4, 16, 256), (4, 4, 16, 256), (4, 4, 16, 256), (4, 4, 16, 256), (16, 16, 128), (16, 16, 128),
            (256, 256),
        )
    ]
    vmem = pl.BlockSpec(memory_space=pltpu.VMEM)
    anywhere = pl.BlockSpec(memory_space=pl.ANY)
    return pl.pallas_call(
        kernel,
        out_shape=(
            jax.ShapeDtypeStruct(centroids.shape, BF),
            jax.ShapeDtypeStruct(inserts.shape, BF),
        ),
        in_specs=[vmem, vmem, vmem, anywhere, anywhere],
        out_specs=(anywhere, vmem),
        scratch_shapes=blocks
        + work
        + back
        + [
            pltpu.SemaphoreType.DMA((STAGES,)),
            pltpu.SemaphoreType.DMA((STAGES,)),
            pltpu.SemaphoreType.DMA((3,)),
        ],
        compiler_params=pltpu.CompilerParams(
            collective_id=0, has_side_effects=True, vmem_limit_bytes=48 * 1024 * 1024
        ),
        cost_estimate=pl.CostEstimate(flops=4_000_000_000, bytes_accessed=8_000_000, transcendentals=0),
    )(list_ids.reshape(1, 128), inserts, prior_counts.reshape(8, 128), centroids, rotation)


def solution(mesh):
    placed = (
        P(("replica", "lists"), None),
        P(("replica", "lists")),
        P("lists", None),
        P("lists"),
        P(),
    )
    return jax.shard_map(
        per_device,
        mesh=mesh,
        in_specs=placed,
        out_specs=(P("lists", None), P(("replica", "lists"), None)),
        check_vma=False,
    )
```

```python
import jax
import jax.numpy as jnp
from jax import lax
from jax.experimental import pallas as pl
from jax.experimental.pallas import tpu as pltpu
from jax.sharding import PartitionSpec as P

MESH = pl.DeviceIdType.MESH
BF = jnp.bfloat16
F32 = jnp.float32
I32 = jnp.int32
STAGES = 21


def mm(a, b):
    return jnp.dot(a, b, preferred_element_type=F32)


def iota(shape, dim):
    return lax.broadcasted_iota(I32, shape, dim)


def onehot(mask):
    return jnp.where(mask, 1.0, 0.0).astype(BF)


def owner_at(zz, gg):
    return (zz << 4) + ((gg & 3) << 2) + (gg >> 2)


def wait_bytes(ref, sem):
    pltpu.make_async_copy(ref, ref, sem).wait()


def kernel(
    ids_hbm, x_hbm, prior_hbm, cent_hbm, rot_hbm, newc_hbm, out_ref,
    ids_ref, x_ref, prior_ref, hbuf, hr, abuf, ra, bbuf, rb1, a2, ra2, b2, rb2, hot_a, hot_b, idb,
    w, wt, cnt, rinv, cvm, rvm, nvm, acc,
    ga, gb, gha, ghb, rga, rgb, rha, rhb, fa, fb, rfa, rfb,
    h2a, h2b, rh2a, rh2b, ht, rht, perm, send, recv, local,
):
    c = lax.axis_index("replica")
    li = lax.axis_index("lists")
    z = li // 16
    x = (li // 4) % 4
    y = li % 4
    zc = z * 2 + c
    g = y * 4 + x


    moved_by = {
        0: [ra.at[pl.ds(0, 15)]], 20: [hr.at[pl.ds(0, 15)]], 1: [bbuf.at[pl.ds(0, 15)]], 2: [a2.at[pl.ds(0, 15)]], 3: [b2.at[pl.ds(0, 15)]],
        4: [hot_a.at[:, 0, pl.ds(0, 3)]], 5: [hot_a.at[:, pl.ds(0, 3)]], 6: [hot_b.at[:, 0, pl.ds(0, 3)]],
        7: [hot_b.at[:, :, pl.ds(0, 3)]], 8: [idb.at[0, pl.ds(0, 3)]], 9: [idb.at[pl.ds(0, 3)]],
        10: [ga.at[pl.ds(0, 15)]], 11: [gb.at[pl.ds(0, 15)]], 12: [gha.at[:, pl.ds(0, 3)]], 13: [ghb.at[:, :, pl.ds(0, 3)]],
        14: [fa.at[pl.ds(0, 15)]], 15: [fb.at[pl.ds(0, 15)]], 16: [h2a.at[:, pl.ds(0, 3)]], 17: [h2b.at[:, pl.ds(0, 3)]],
        18: [ht.at[pl.ds(0, 15)]], 19: [nvm],
    }
    started, arrived = [], []

    def arrive(stage):
        arrived.append(stage)
        for ref in moved_by[stage]:
            wait_bytes(ref, recv.at[stage])

    def finish():
        for stage in dict.fromkeys(started):
            if stage not in arrived:
                arrive(stage)
            for ref in moved_by[stage]:
                wait_bytes(ref, send.at[stage])

    def dev(zc_to, g_to):
        return (zc_to % 2, (zc_to // 2) * 16 + (g_to % 4) * 4 + g_to // 4)

    def start(stage, src, dst, zc_to, g_to):
        started.append(stage)
        pltpu.make_async_remote_copy(
            src_ref=src, dst_ref=dst, send_sem=send.at[stage], recv_sem=recv.at[stage],
            device_id=dev(zc_to, g_to), device_id_type=MESH,
        ).start()

    def along_zc(stage, src, dst):
        @pl.loop(1, 16)
        def _(step):
            to = (zc + step) % 16
            start(stage, src.at[to], dst.at[zc], to, g)

    def along_g(stage, src, dst):
        @pl.loop(1, 16)
        def _(step):
            to = (g + step) % 16
            start(stage, src.at[to], dst.at[g], zc, to)

    barrier = pltpu.get_barrier_semaphore()

    @pl.loop(1, 16)
    def _(step):
        pl.semaphore_signal(barrier, 1, device_id=dev((zc + step) % 16, g), device_id_type=MESH)
        pl.semaphore_signal(barrier, 1, device_id=dev(zc, (g + step) % 16), device_id_type=MESH)

    half = pl.ds(pl.multiple_of(c * 512, 512), 512)
    copies = [
        pltpu.make_async_copy(src, dst, local.at[n])
        for n, (src, dst) in enumerate(
            ((ids_hbm, ids_ref), (x_hbm, x_ref), (prior_hbm, prior_ref), (cent_hbm.at[:, half], cvm), (rot_hbm, rvm))
        )
    ]
    for copy in copies:
        copy.start()
    copies[0].wait()

    ids = ids_ref[...]
    owner_row = ids >> 10
    eye = iota((128, 128), 0) == iota((128, 128), 1)
    owner_col = jnp.sum(jnp.where(eye, owner_row, 0), axis=1, keepdims=True)
    same = jnp.where(owner_col == owner_row, 1.0, 0.0)
    earlier = jnp.where(iota((128, 128), 0) < iota((128, 128), 1), same, 0.0)
    later = jnp.where(iota((128, 128), 1) < iota((128, 128), 0), same, 0.0)
    rank_row = jnp.sum(earlier, axis=0, keepdims=True)
    rank_col = jnp.sum(later, axis=1, keepdims=True)
    cold_owner_row = jnp.where(rank_row > 0.5, -1, owner_row)
    cold_owner_col = jnp.where(rank_col > 0.5, -1, owner_col)

    tile_row = iota((16, 128), 0)
    info = jnp.where(tile_row == 12, owner_row, 0)
    info = jnp.where(tile_row == 13, (ids & 1023) >> 5, info)
    info = jnp.where(tile_row == 14, ids & 31, info).astype(F32)
    info = jnp.where(tile_row == 15, rank_row, info)
    copies[1].wait()
    for cc in range(2):
        tile = info
        for j in range(4):
            match = (tile_row >= j * 3) & (tile_row < j * 3 + 3) & ((tile_row - (j * 3 - 1)).astype(F32) == rank_row)
            low = cc * 512 + j * 128
            tile = tile + mm(onehot(match), x_ref[:, low : low + 128])
        hbuf[cc] = tile.astype(BF)
    p0, p1 = iota((256, 256), 0), iota((256, 256), 1)
    perm[...] = onehot((p0 >> 4 == p1 & 15) & (p0 & 15 == p1 >> 4))

    def swap(rows):
        return mm(perm[...], rows).astype(BF)

    hr[zc] = hbuf[c]
    pl.semaphore_wait(barrier, 30)

    @pl.loop(1, 16)
    def _(step):
        to = (zc + step) % 16
        start(20, hbuf.at[to % 2], hr.at[zc], to, g)

    r128 = iota((128, 128), 0)
    pick = onehot(owner_at(r128 >> 4, r128 & 15) == cold_owner_row)
    for cc in range(2):
        block = mm(pick, x_ref[:, cc * 512 : cc * 512 + 256]).astype(BF)
        abuf[:, cc] = block.reshape(8, 16, 256)
    ra[zc] = abuf[z, c]

    @pl.loop(1, 16)
    def _(step):
        to = (zc + step) % 16
        start(0, abuf.at[to // 2, to % 2], ra.at[zc], to, g)

    r256 = iota((256, 128), 0)
    hit = owner_at((r256 & 15) >> 1, r256 >> 4) == cold_owner_row
    part_b = mm(onehot(hit & ((r256 & 1) == 0)), x_ref[:, 256:512])
    part_b = part_b + mm(onehot(hit & ((r256 & 1) == 1)), x_ref[:, 768:1024])
    bbuf[...] = part_b.astype(BF).reshape(16, 16, 256)
    rb1[g] = bbuf[g]
    along_g(1, bbuf, rb1)

    copies[2].wait()
    ones = jnp.ones((128, 128), BF)
    for a in range(8):
        diag = jnp.where(eye, prior_ref[a : a + 1, :].astype(F32), 0.0).astype(BF)
        rinv[a * 128 : a * 128 + 128, :] = mm(diag, ones)

    arrive(20)
    hot_rows = mm(perm[...], hr[...].reshape(256, 128))
    hot = hot_rows.astype(BF)
    for j, (ref, low) in enumerate(((hot_a, 0), (hot_a, 128), (hot_b, 0), (hot_b, 128))):
        ref[:, y, x, :, low : low + 128] = hot[j * 48 : j * 48 + 48].reshape(3, 16, 128)
    got = hot_rows[192:256].astype(I32)
    idb[y, x] = (got[48:64] << 17) + (got[0:16] << 10) + (got[16:32] << 5) + got[32:48]
    for step in range(1, 4):
        to = y * 4 + (x + step) % 4
        start(8, idb.at[y, x], idb.at[y, x], zc, to)
        start(4, hot_a.at[:, y, x], hot_a.at[:, y, x], zc, to)
        start(6, hot_b.at[:, y, x], hot_b.at[:, y, x], zc, ((y + step) % 4) * 4 + x)

    arrive(0)
    a2[...] = swap(ra[...].reshape(256, 256)).reshape(16, 16, 256)
    ra2[g] = a2[g]
    along_g(2, a2, ra2)

    arrive(1)
    b2[...] = swap(rb1[...].reshape(256, 256)).reshape(16, 16, 256)
    rb2[zc] = b2[zc]
    along_zc(3, b2, rb2)

    arrive(8)
    arrive(4)
    arrive(6)
    for step in range(1, 4):
        to = ((y + step) % 4) * 4 + x
        start(9, idb.at[y], idb.at[y], zc, to)
        start(5, hot_a.at[:, y], hot_a.at[:, y], zc, to)
        start(7, hot_b.at[:, :, x], hot_b.at[:, :, x], zc, y * 4 + (x + step) % 4)

    arrive(9)
    code = idb[...].reshape(256, 128)
    mine = ((code >> 10) & 127) == li
    slot = code >> 17
    number = (code & 1023) + 1
    ones8 = jnp.ones((8, 256), BF)
    ones256 = jnp.ones((256, 128), BF)
    for block, s in enumerate((0, 1, 2, 3)):
        here = mine & (slot == s)
        top = jnp.where(here, number & 2016, 0).astype(F32).astype(BF)
        low = jnp.where(here, number & 31, 0).astype(F32).astype(BF)
        both = jnp.concatenate([top, low], axis=1)
        lanes = lax.dot_general(ones8, both, (((1,), (1,)), ((), ())), preferred_element_type=F32)
        lanes = lanes.astype(I32)[0:1, :] - 1
        rows = mm(both, ones256).astype(I32) - 1
        for a in range(8):
            w[a * 128 : a * 128 + 128, block * 256 : block * 256 + 256] = onehot(
                iota((128, 256), 0) + a * 128 == lanes
            )
            wt[block * 256 : block * 256 + 256, a * 128 : a * 128 + 128] = onehot(
                iota((256, 128), 1) + a * 128 == rows
            )
    for a in range(4):
        lists = slice(a * 256, a * 256 + 256)
        total = mm(w[lists, :], jnp.ones((1024, 128), BF))
        cnt[lists, :] = total
        rinv[lists, :] = 1.0 / (rinv[lists, :] + total)

    def begin(part, cold):
        for a in range(4):
            lists = slice(a * 256, a * 256 + 256)
            old = cvm[lists, part * 256 : part * 256 + 256].astype(F32)
            count = jnp.concatenate([cnt[lists, :]] * 2, axis=1)
            acc[part, lists, :] = mm(w[lists, 0:256], cold) - count * old

    def refresh(part, hot_rows):
        cols = slice(part * 256, part * 256 + 256)
        for a in range(4):
            lists = slice(a * 256, a * 256 + 256)
            change = acc[part, lists, :] + mm(w[lists, 256:1024], hot_rows)
            scale = jnp.concatenate([rinv[lists, :]] * 2, axis=1)
            nvm[lists, cols] = (cvm[lists, cols].astype(F32) + change * scale).astype(BF)
        return nvm[:, cols]

    copies[3].wait()
    arrive(2)
    begin(0, ra2[...].reshape(256, 256))
    arrive(3)
    begin(1, swap(rb2[...].reshape(256, 256)))

    arrive(5)
    new_a = refresh(0, hot_a[...].reshape(768, 256))
    gha[...] = mm(wt[256:1024, :], new_a).astype(BF).reshape(3, 4, 4, 16, 256)
    for step in range(1, 4):
        to = (y + step) % 4
        start(12, gha.at[:, to], rha.at[y], zc, to * 4 + x)
    arrive(7)
    new_b = refresh(1, hot_b[...].reshape(768, 256))
    ghb[...] = mm(wt[256:1024, :], new_b).astype(BF).reshape(3, 4, 4, 16, 256)
    for step in range(1, 4):
        to = (x + step) % 4
        start(13, ghb.at[:, :, to], rhb.at[x], zc, y * 4 + to)
    ga[...] = mm(wt[0:256, :], new_a).astype(BF).reshape(16, 16, 256)
    rga[g] = ga[g]
    along_g(10, ga, rga)
    gb[...] = swap(mm(wt[0:256, :], new_b).astype(BF)).reshape(16, 16, 256)
    rgb[zc] = gb[zc]
    along_zc(11, gb, rgb)
    rha[y] = gha[:, y]
    rhb[x] = ghb[:, :, x]

    start(19, nvm, newc_hbm.at[:, half], zc + 1 - 2 * c, g)
    own_copy = pltpu.make_async_copy(nvm, newc_hbm.at[:, half], local.at[5])
    own_copy.start()

    arrive(12)
    h2a[...] = (rha[0] + rha[1]) + (rha[2] + rha[3])
    for step in range(1, 4):
        to = (x + step) % 4
        start(16, h2a.at[:, to], rh2a.at[x], zc, y * 4 + to)
    rh2a[x] = h2a[:, x]
    arrive(13)
    h2b[...] = (rhb[0] + rhb[1]) + (rhb[2] + rhb[3])
    for step in range(1, 4):
        to = (y + step) % 4
        start(17, h2b.at[:, to], rh2b.at[y], zc, to * 4 + x)
    rh2b[y] = h2b[:, y]

    arrive(10)
    fa[...] = swap(rga[...].reshape(256, 256)).reshape(16, 16, 256)
    rfa[zc] = fa[zc]
    along_zc(14, fa, rfa)
    arrive(11)
    fb[...] = swap(rgb[...].reshape(256, 256)).reshape(16, 16, 256)
    rfb[g] = fb[g]
    along_g(15, fb, rfb)

    arrive(16)
    arrive(17)
    back_a = ((rh2a[0] + rh2a[1]) + (rh2a[2] + rh2a[3])).reshape(48, 256)
    back_b = ((rh2b[0] + rh2b[1]) + (rh2b[2] + rh2b[3])).reshape(48, 256)
    back = jnp.concatenate(
        [back_a[:, :128], back_a[:, 128:], back_b[:, :128], back_b[:, 128:], jnp.zeros((64, 128), BF)], axis=0
    )
    ht[...] = swap(back).reshape(16, 16, 128)
    rht[zc] = ht[zc]
    along_zc(18, ht, rht)

    lane = iota((128, 256), 1)
    hit_a = owner_at(lane >> 5, lane & 15) == cold_owner_col
    hit_b = owner_at((lane & 15) >> 1, lane >> 4) == cold_owner_col
    arrive(14)
    arrive(15)
    picked = []
    for cc in range(2):
        picked.append(mm(onehot(hit_a & ((lane >> 4) & 1 == cc)), rfa[...].reshape(256, 256)))
        picked.append(mm(onehot(hit_b & (lane & 1 == cc)), rfb[...].reshape(256, 256)))
    arrive(18)
    tile_lane = iota((128, 16), 1)
    tiles = []
    for cc in range(2):
        tile = rht[cc]
        for zz in range(1, 8):
            tile = tile + rht[zz * 2 + cc]
        for j in range(4):
            match = (tile_lane >= j * 3) & (tile_lane < j * 3 + 3) & ((tile_lane - (j * 3 - 1)).astype(F32) == rank_col)
            tiles.append(mm(onehot(match), tile))
    near = jnp.concatenate(picked, axis=1) + jnp.concatenate(tiles, axis=1)
    residual = (x_ref[...].astype(F32) - near).astype(BF)
    copies[4].wait()
    for a in range(4):
        cols = slice(a * 256, a * 256 + 256)
        out_ref[:, cols] = mm(residual, rvm[:, cols]).astype(BF)

    own_copy.wait()
    finish()


def per_device(inserts, list_ids, centroids, prior_counts, rotation):
    square, tall, plane = (16, 16, 256), (3, 4, 4, 16, 256), (4, 3, 16, 256)
    shapes = [
        (2, 16, 128), (16, 16, 128), (8, 2, 16, 256), square, square, square, square, square, square, square, tall, tall,
        None, (1024, 1024), (1024, 1024), None, None, (1024, 512), (1024, 1024), (1024, 512), None,
        square, square, tall, tall, square, square, (4, 3, 4, 16, 256), (4, 3, 4, 16, 256), square, square, square, square,
        (3, 4, 16, 256), (3, 4, 16, 256), plane, plane, (16, 16, 128), (16, 16, 128), (256, 256),
    ]
    others = [
        pltpu.VMEM((4, 4, 16, 128), I32),
        pltpu.VMEM((1024, 128), F32),
        pltpu.VMEM((1024, 128), F32),
        pltpu.VMEM((2, 1024, 256), F32),
    ]
    scratch = [pltpu.VMEM(shape, BF) if shape else others.pop(0) for shape in shapes]
    given = [pltpu.VMEM((1, 128), I32), pltpu.VMEM(inserts.shape, BF), pltpu.VMEM((8, 128), I32)]
    vmem = pl.BlockSpec(memory_space=pltpu.VMEM)
    anywhere = pl.BlockSpec(memory_space=pl.ANY)
    return pl.pallas_call(
        kernel,
        out_shape=(
            jax.ShapeDtypeStruct(centroids.shape, BF),
            jax.ShapeDtypeStruct(inserts.shape, BF),
        ),
        in_specs=[pl.BlockSpec(memory_space=pltpu.HBM)] * 5,
        out_specs=(anywhere, vmem),
        scratch_shapes=given
        + scratch
        + [
            pltpu.SemaphoreType.DMA((STAGES,)),
            pltpu.SemaphoreType.DMA((STAGES,)),
            pltpu.SemaphoreType.DMA((6,)),
        ],
        compiler_params=pltpu.CompilerParams(
            collective_id=0, has_side_effects=True, vmem_limit_bytes=48 * 1024 * 1024
        ),
        cost_estimate=pl.CostEstimate(flops=4_000_000_000, bytes_accessed=8_000_000, transcendentals=0),
    )(list_ids.reshape(1, 128), inserts, prior_counts.reshape(8, 128), centroids, rotation)


def solution(mesh):
    placed = (
        P(("replica", "lists"), None),
        P(("replica", "lists")),
        P("lists", None),
        P("lists"),
        P(),
    )
    return jax.shard_map(
        per_device,
        mesh=mesh,
        in_specs=placed,
        out_specs=(P("lists", None), P(("replica", "lists"), None)),
        check_vma=False,
    )
```

```python
import jax
import jax.numpy as jnp
from jax import lax
from jax.experimental import pallas as pl
from jax.experimental.pallas import tpu as pltpu
from jax.sharding import PartitionSpec as P

MESH = pl.DeviceIdType.MESH
BF = jnp.bfloat16
F32 = jnp.float32
I32 = jnp.int32
STAGES = 21


def mm(a, b):
    return jnp.dot(a, b, preferred_element_type=F32)


def iota(shape, dim):
    return lax.broadcasted_iota(I32, shape, dim)


def onehot(mask):
    return jnp.where(mask, 1.0, 0.0).astype(BF)


def owner_at(zz, gg):
    return (zz << 4) + ((gg & 3) << 2) + (gg >> 2)


def wait_bytes(ref, sem):
    pltpu.make_async_copy(ref, ref, sem).wait()


def kernel(
    ids_hbm, x_hbm, prior_hbm, cent_hbm, rot_hbm, newc_hbm, out_ref,
    ids_ref, x_ref, prior_ref, hbuf, hr, abuf, ra, bbuf, rb1, a2, ra2, b2, rb2, hot_a, hot_b, idb,
    w, wt, mates, crow, prior_of, rowsb, nrow, irow, cvm, rvm, nvm, acc,
    ga, gb, gha, ghb, rga, rgb, rha, rhb, fa, fb, rfa, rfb,
    h2a, h2b, rh2a, rh2b, ht, rht, perm, send, recv, local,
):
    c = lax.axis_index("replica")
    li = lax.axis_index("lists")
    z = li // 16
    x = (li // 4) % 4
    y = li % 4
    zc = z * 2 + c
    g = y * 4 + x


    moved_by = {
        0: [ra.at[pl.ds(0, 15)]], 20: [hr.at[pl.ds(0, 15)]], 1: [bbuf.at[pl.ds(0, 15)]], 2: [a2.at[pl.ds(0, 15)]], 3: [b2.at[pl.ds(0, 15)]],
        4: [hot_a.at[:, 0, pl.ds(0, 3)]], 5: [hot_a.at[:, pl.ds(0, 3)]], 6: [hot_b.at[:, 0, pl.ds(0, 3)]],
        7: [hot_b.at[:, :, pl.ds(0, 3)]], 8: [idb.at[pl.ds(0, 15)]],
        10: [ga.at[pl.ds(0, 15)]], 11: [gb.at[pl.ds(0, 15)]], 12: [gha.at[:, pl.ds(0, 3)]], 13: [ghb.at[:, :, pl.ds(0, 3)]],
        14: [fa.at[pl.ds(0, 15)]], 15: [fb.at[pl.ds(0, 15)]], 16: [h2a.at[:, pl.ds(0, 3)]], 17: [h2b.at[:, pl.ds(0, 3)]],
        18: [ht.at[pl.ds(0, 15)]], 19: [nvm],
    }
    started, arrived = [], []

    def arrive(stage):
        arrived.append(stage)
        for ref in moved_by[stage]:
            wait_bytes(ref, recv.at[stage])

    def finish():
        for stage in dict.fromkeys(started):
            if stage not in arrived:
                arrive(stage)
            for ref in moved_by[stage]:
                wait_bytes(ref, send.at[stage])

    def dev(zc_to, g_to):
        return (zc_to % 2, (zc_to // 2) * 16 + (g_to % 4) * 4 + g_to // 4)

    def start(stage, src, dst, zc_to, g_to):
        started.append(stage)
        pltpu.make_async_remote_copy(
            src_ref=src, dst_ref=dst, send_sem=send.at[stage], recv_sem=recv.at[stage],
            device_id=dev(zc_to, g_to), device_id_type=MESH,
        ).start()

    def along_zc(stage, src, dst):
        @pl.loop(1, 16)
        def _(step):
            to = (zc + step) % 16
            start(stage, src.at[to], dst.at[zc], to, g)

    def along_g(stage, src, dst):
        @pl.loop(1, 16)
        def _(step):
            to = (g + step) % 16
            start(stage, src.at[to], dst.at[g], zc, to)

    barrier = pltpu.get_barrier_semaphore()

    @pl.loop(1, 16)
    def _(step):
        pl.semaphore_signal(barrier, 1, device_id=dev((zc + step) % 16, g), device_id_type=MESH)
        pl.semaphore_signal(barrier, 1, device_id=dev(zc, (g + step) % 16), device_id_type=MESH)

    half = pl.ds(pl.multiple_of(c * 512, 512), 512)
    copies = [
        pltpu.make_async_copy(src, dst, local.at[n])
        for n, (src, dst) in enumerate(
            ((ids_hbm, ids_ref), (x_hbm, x_ref), (prior_hbm, prior_ref), (cent_hbm.at[:, half], cvm), (rot_hbm, rvm))
        )
    ]
    for copy in copies:
        copy.start()
    copies[0].wait()

    ids = ids_ref[...]
    owner_row = ids >> 10
    eye = iota((128, 128), 0) == iota((128, 128), 1)
    owner_col = jnp.sum(jnp.where(eye, owner_row, 0), axis=1, keepdims=True)
    same = jnp.where(owner_col == owner_row, 1.0, 0.0)
    earlier = jnp.where(iota((128, 128), 0) < iota((128, 128), 1), same, 0.0)
    later = jnp.where(iota((128, 128), 1) < iota((128, 128), 0), same, 0.0)
    rank_row = jnp.sum(earlier, axis=0, keepdims=True)
    rank_col = jnp.sum(later, axis=1, keepdims=True)
    cold_owner_row = jnp.where(rank_row > 0.5, -1, owner_row)
    cold_owner_col = jnp.where(rank_col > 0.5, -1, owner_col)

    tile_row = iota((16, 128), 0)
    info = jnp.where(tile_row == 12, owner_row, 0)
    info = jnp.where(tile_row == 13, (ids & 1023) >> 5, info)
    info = jnp.where(tile_row == 14, ids & 31, info).astype(F32)
    info = jnp.where(tile_row == 15, rank_row, info)
    copies[1].wait()
    for cc in range(2):
        tile = info
        for j in range(4):
            match = (tile_row >= j * 3) & (tile_row < j * 3 + 3) & ((tile_row - (j * 3 - 1)).astype(F32) == rank_row)
            low = cc * 512 + j * 128
            tile = tile + mm(onehot(match), x_ref[:, low : low + 128])
        hbuf[cc] = tile.astype(BF)
    p0, p1 = iota((256, 256), 0), iota((256, 256), 1)
    perm[...] = onehot((p0 >> 4 == p1 & 15) & (p0 & 15 == p1 >> 4))

    def swap(rows):
        return mm(perm[...], rows).astype(BF)

    hr[zc] = hbuf[c]
    pl.semaphore_wait(barrier, 30)

    @pl.loop(1, 16)
    def _(step):
        to = (zc + step) % 16
        start(20, hbuf.at[to % 2], hr.at[zc], to, g)

    r128 = iota((128, 128), 0)
    pick = onehot(owner_at(r128 >> 4, r128 & 15) == cold_owner_row)
    for cc in range(2):
        block = mm(pick, x_ref[:, cc * 512 : cc * 512 + 256]).astype(BF)
        abuf[:, cc] = block.reshape(8, 16, 256)
    ra[zc] = abuf[z, c]

    @pl.loop(1, 16)
    def _(step):
        to = (zc + step) % 16
        start(0, abuf.at[to // 2, to % 2], ra.at[zc], to, g)

    r256 = iota((256, 128), 0)
    hit = owner_at((r256 & 15) >> 1, r256 >> 4) == cold_owner_row
    part_b = mm(onehot(hit & ((r256 & 1) == 0)), x_ref[:, 256:512])
    part_b = part_b + mm(onehot(hit & ((r256 & 1) == 1)), x_ref[:, 768:1024])
    bbuf[...] = part_b.astype(BF).reshape(16, 16, 256)
    rb1[g] = bbuf[g]
    along_g(1, bbuf, rb1)

    copies[2].wait()
    ones = jnp.ones((128, 128), BF)
    for a in range(8):
        diag = jnp.where(eye, prior_ref[a : a + 1, :].astype(F32), 0.0).astype(BF)
        prior_of[a * 128 : a * 128 + 128, :] = mm(diag, ones).astype(BF)

    arrive(20)
    hot_rows = mm(perm[...], hr[...].reshape(256, 128))
    hot = hot_rows.astype(BF)
    for j, (ref, low) in enumerate(((hot_a, 0), (hot_a, 128), (hot_b, 0), (hot_b, 128))):
        ref[:, y, x, :, low : low + 128] = hot[j * 48 : j * 48 + 48].reshape(3, 16, 128)
    got = hot_rows[192:256].astype(I32)
    idb[g] = (got[48:64] << 17) + (got[0:16] << 10) + (got[16:32] << 5) + got[32:48]

    @pl.loop(1, 16)
    def _(step):
        start(8, idb.at[g], idb.at[g], zc, (g + step) % 16)

    for step in range(1, 4):
        to = y * 4 + (x + step) % 4
        start(4, hot_a.at[:, y, x], hot_a.at[:, y, x], zc, to)
        start(6, hot_b.at[:, y, x], hot_b.at[:, y, x], zc, ((y + step) % 4) * 4 + x)

    arrive(0)
    a2[...] = swap(ra[...].reshape(256, 256)).reshape(16, 16, 256)
    ra2[g] = a2[g]
    along_g(2, a2, ra2)

    arrive(1)
    b2[...] = swap(rb1[...].reshape(256, 256)).reshape(16, 16, 256)
    rb2[zc] = b2[zc]
    along_zc(3, b2, rb2)

    arrive(4)
    arrive(6)
    for step in range(1, 4):
        to = ((y + step) % 4) * 4 + x
        start(5, hot_a.at[:, y], hot_a.at[:, y], zc, to)
        start(7, hot_b.at[:, :, x], hot_b.at[:, :, x], zc, y * 4 + (x + step) % 4)

    arrive(8)
    code = idb[...].reshape(256, 128)
    mine = ((code >> 10) & 127) == li
    rank = code >> 17
    number = (code & 1023) + 1
    ones8 = jnp.ones((8, 256), BF)
    ones256 = jnp.ones((256, 128), BF)
    lanes, rows = [], []
    for s in range(4):
        here = mine & (rank == s)
        top = jnp.where(here, number & 2016, 0).astype(F32).astype(BF)
        low = jnp.where(here, number & 31, 0).astype(F32).astype(BF)
        both = jnp.concatenate([top, low], axis=1)
        lane = lax.dot_general(ones8, both, (((1,), (1,)), ((), ())), preferred_element_type=F32)
        lane = lane.astype(I32)[0:1, :]
        lanes.append(jnp.where(lane == 0, -2, lane - 1))
        rows.append(mm(both, ones256).astype(I32) - 1)
    copies[3].wait()
    for s in range(4):
        block = slice(s * 256, s * 256 + 256)
        for a in range(8):
            wt[block, a * 128 : a * 128 + 128] = onehot(iota((256, 128), 1) + a * 128 == rows[s])
        for t in range(4):
            for h in range(2):
                low = t * 256 + h * 128
                mates[block, low : low + 128] = onehot(rows[s] == lanes[t][:, h * 128 : h * 128 + 128])
        crow[block, :] = mm(wt[block, :], cvm[...]).astype(BF)
        total = mm(mates[block, :], jnp.ones((1024, 128), BF))
        nrow[block, :] = total
        irow[block, :] = 1.0 / jnp.maximum(mm(wt[block, :], prior_of[...]) + total, 1.0)

    def twice(rows128):
        return jnp.concatenate([rows128] * 2, axis=1)

    def begin(part, cold):
        cols = slice(part * 256, part * 256 + 256)
        for a in range(4):
            block = slice(a * 256, a * 256 + 256)
            acc[part, block, :] = mm(mates[block, 0:256], cold) - twice(nrow[block, :]) * crow[block, cols].astype(F32)

    def near_rows(part, a, hot_rows):
        block = slice(a * 256, a * 256 + 256)
        change = acc[part, block, :] + mm(mates[block, 256:1024], hot_rows)
        return (crow[block, part * 256 : part * 256 + 256].astype(F32) + change * twice(irow[block, :])).astype(BF)

    arrive(2)
    begin(0, ra2[...].reshape(256, 256))
    arrive(3)
    rowsb[...] = swap(rb2[...].reshape(256, 256))
    begin(1, rowsb[...])

    arrive(5)
    for k in range(3):
        gha[k] = near_rows(0, k + 1, hot_a[...].reshape(768, 256)).reshape(4, 4, 16, 256)
    for step in range(1, 4):
        to = (y + step) % 4
        start(12, gha.at[:, to], rha.at[y], zc, to * 4 + x)
    arrive(7)
    for k in range(3):
        ghb[k] = near_rows(1, k + 1, hot_b[...].reshape(768, 256)).reshape(4, 4, 16, 256)
    for step in range(1, 4):
        to = (x + step) % 4
        start(13, ghb.at[:, :, to], rhb.at[x], zc, y * 4 + to)
    ga[...] = near_rows(0, 0, hot_a[...].reshape(768, 256)).reshape(16, 16, 256)
    rga[g] = ga[g]
    along_g(10, ga, rga)
    gb[...] = swap(near_rows(1, 0, hot_b[...].reshape(768, 256))).reshape(16, 16, 256)
    rgb[zc] = gb[zc]
    along_zc(11, gb, rgb)
    rha[y] = gha[:, y]
    rhb[x] = ghb[:, :, x]

    for t in range(4):
        for a in range(8):
            w[a * 128 : a * 128 + 128, t * 256 : t * 256 + 256] = onehot(iota((128, 256), 0) + a * 128 == lanes[t])

    arrive(12)
    h2a[...] = (rha[0] + rha[1]) + (rha[2] + rha[3])
    for step in range(1, 4):
        to = (x + step) % 4
        start(16, h2a.at[:, to], rh2a.at[x], zc, y * 4 + to)
    rh2a[x] = h2a[:, x]
    arrive(13)
    h2b[...] = (rhb[0] + rhb[1]) + (rhb[2] + rhb[3])
    for step in range(1, 4):
        to = (y + step) % 4
        start(17, h2b.at[:, to], rh2b.at[y], zc, to * 4 + x)
    rh2b[y] = h2b[:, y]

    arrive(10)
    fa[...] = swap(rga[...].reshape(256, 256)).reshape(16, 16, 256)
    rfa[zc] = fa[zc]
    along_zc(14, fa, rfa)
    arrive(11)
    fb[...] = swap(rgb[...].reshape(256, 256)).reshape(16, 16, 256)
    rfb[g] = fb[g]
    along_g(15, fb, rfb)

    for a in range(4):
        lists = slice(a * 256, a * 256 + 256)
        count = mm(w[lists, :], jnp.ones((1024, 128), BF))
        scale = twice(1.0 / (prior_of[lists, :].astype(F32) + count))
        for part, (cold, hot_rows) in enumerate(((ra2[...].reshape(256, 256), hot_a), (rowsb[...], hot_b))):
            cols = slice(part * 256, part * 256 + 256)
            old = cvm[lists, cols].astype(F32)
            sums = mm(w[lists, 0:256], cold) + mm(w[lists, 256:1024], hot_rows[...].reshape(768, 256))
            nvm[lists, cols] = (old + (sums - twice(count) * old) * scale).astype(BF)
    start(19, nvm, newc_hbm.at[:, half], zc + 1 - 2 * c, g)
    own_copy = pltpu.make_async_copy(nvm, newc_hbm.at[:, half], local.at[5])
    own_copy.start()

    arrive(16)
    arrive(17)
    back_a = ((rh2a[0] + rh2a[1]) + (rh2a[2] + rh2a[3])).reshape(48, 256)
    back_b = ((rh2b[0] + rh2b[1]) + (rh2b[2] + rh2b[3])).reshape(48, 256)
    back = jnp.concatenate(
        [back_a[:, :128], back_a[:, 128:], back_b[:, :128], back_b[:, 128:], jnp.zeros((64, 128), BF)], axis=0
    )
    ht[...] = swap(back).reshape(16, 16, 128)
    rht[zc] = ht[zc]
    along_zc(18, ht, rht)

    lane = iota((128, 256), 1)
    hit_a = owner_at(lane >> 5, lane & 15) == cold_owner_col
    hit_b = owner_at((lane & 15) >> 1, lane >> 4) == cold_owner_col
    arrive(14)
    arrive(15)
    picked = []
    for cc in range(2):
        picked.append(mm(onehot(hit_a & ((lane >> 4) & 1 == cc)), rfa[...].reshape(256, 256)))
        picked.append(mm(onehot(hit_b & (lane & 1 == cc)), rfb[...].reshape(256, 256)))
    arrive(18)
    tile_lane = iota((128, 16), 1)
    tiles = []
    for cc in range(2):
        tile = rht[cc]
        for zz in range(1, 8):
            tile = tile + rht[zz * 2 + cc]
        for j in range(4):
            match = (tile_lane >= j * 3) & (tile_lane < j * 3 + 3) & ((tile_lane - (j * 3 - 1)).astype(F32) == rank_col)
            tiles.append(mm(onehot(match), tile))
    near = jnp.concatenate(picked, axis=1) + jnp.concatenate(tiles, axis=1)
    residual = (x_ref[...].astype(F32) - near).astype(BF)
    copies[4].wait()
    for a in range(4):
        cols = slice(a * 256, a * 256 + 256)
        out_ref[:, cols] = mm(residual, rvm[:, cols]).astype(BF)

    own_copy.wait()
    finish()


def per_device(inserts, list_ids, centroids, prior_counts, rotation):
    square, tall, plane = (16, 16, 256), (3, 4, 4, 16, 256), (4, 3, 16, 256)
    shapes = [
        (2, 16, 128), (16, 16, 128), (8, 2, 16, 256), square, square, square, square, square, square, square, tall, tall,
        None, (1024, 1024), (1024, 1024), (1024, 1024), (1024, 512), (1024, 128), (256, 256), None, None, (1024, 512), (1024, 1024), (1024, 512), None,
        square, square, tall, tall, square, square, (4, 3, 4, 16, 256), (4, 3, 4, 16, 256), square, square, square, square,
        (3, 4, 16, 256), (3, 4, 16, 256), plane, plane, (16, 16, 128), (16, 16, 128), (256, 256),
    ]
    others = [
        pltpu.VMEM((16, 16, 128), I32),
        pltpu.VMEM((1024, 128), F32),
        pltpu.VMEM((1024, 128), F32),
        pltpu.VMEM((2, 1024, 256), F32),
    ]
    scratch = [pltpu.VMEM(shape, BF) if shape else others.pop(0) for shape in shapes]
    given = [pltpu.VMEM((1, 128), I32), pltpu.VMEM(inserts.shape, BF), pltpu.VMEM((8, 128), I32)]
    vmem = pl.BlockSpec(memory_space=pltpu.VMEM)
    anywhere = pl.BlockSpec(memory_space=pl.ANY)
    return pl.pallas_call(
        kernel,
        out_shape=(
            jax.ShapeDtypeStruct(centroids.shape, BF),
            jax.ShapeDtypeStruct(inserts.shape, BF),
        ),
        in_specs=[pl.BlockSpec(memory_space=pltpu.HBM)] * 5,
        out_specs=(anywhere, vmem),
        scratch_shapes=given
        + scratch
        + [
            pltpu.SemaphoreType.DMA((STAGES,)),
            pltpu.SemaphoreType.DMA((STAGES,)),
            pltpu.SemaphoreType.DMA((6,)),
        ],
        compiler_params=pltpu.CompilerParams(
            collective_id=0, has_side_effects=True, vmem_limit_bytes=58 * 1024 * 1024
        ),
        cost_estimate=pl.CostEstimate(flops=4_000_000_000, bytes_accessed=8_000_000, transcendentals=0),
    )(list_ids.reshape(1, 128), inserts, prior_counts.reshape(8, 128), centroids, rotation)


def solution(mesh):
    placed = (
        P(("replica", "lists"), None),
        P(("replica", "lists")),
        P("lists", None),
        P("lists"),
        P(),
    )
    return jax.shard_map(
        per_device,
        mesh=mesh,
        in_specs=placed,
        out_specs=(P("lists", None), P(("replica", "lists"), None)),
        check_vma=False,
    )
```

```python
import jax
import jax.numpy as jnp
from jax import lax
from jax.experimental import pallas as pl
from jax.experimental.pallas import tpu as pltpu
from jax.sharding import PartitionSpec as P

MESH = pl.DeviceIdType.MESH
BF = jnp.bfloat16
F32 = jnp.float32
I32 = jnp.int32
STAGES = 21


def mm(a, b):
    return jnp.dot(a, b, preferred_element_type=F32)


def iota(shape, dim):
    return lax.broadcasted_iota(I32, shape, dim)


def onehot(mask):
    return jnp.where(mask, 1.0, 0.0).astype(BF)


def owner_at(zz, gg):
    return (zz << 4) + ((gg & 3) << 2) + (gg >> 2)


def wait_bytes(ref, sem):
    pltpu.make_async_copy(ref, ref, sem).wait()


def kernel(
    ids_hbm, x_hbm, prior_hbm, cent_hbm, rot_hbm, newc_hbm, out_ref,
    ids_ref, x_ref, prior_ref, hbuf, hr, bbuf, rb1, b2, rb2, hot_a, hot_b, idb,
    w, wt, mates, crow, prior_of, cold, nrow, irow, cvm, rvm, nvm, acc,
    gb, gha, ghb, rgb, rha, rhb, fb, rfb,
    h2a, h2b, rh2a, rh2b, ht, rht, perm, send, recv, local,
):
    c = lax.axis_index("replica")
    li = lax.axis_index("lists")
    z = li // 16
    x = (li // 4) % 4
    y = li % 4
    zc = z * 2 + c
    g = y * 4 + x


    moved_by = {
        20: [hr.at[pl.ds(0, 15)]], 1: [bbuf.at[pl.ds(0, 15)]], 3: [b2.at[pl.ds(0, 15)]], 8: [idb.at[pl.ds(0, 15)]],
        4: [hot_a.at[:, 0, pl.ds(0, 3)]], 5: [hot_a.at[:, pl.ds(0, 3)]], 6: [hot_b.at[:, 0, pl.ds(0, 3)]],
        7: [hot_b.at[:, :, pl.ds(0, 3)]], 11: [gb.at[pl.ds(0, 15)]], 12: [gha.at[:, pl.ds(0, 3)]],
        13: [ghb.at[:, :, pl.ds(0, 3)]], 15: [fb.at[pl.ds(0, 15)]], 16: [h2a.at[:, pl.ds(0, 3)]],
        17: [h2b.at[:, pl.ds(0, 3)]], 18: [ht.at[pl.ds(0, 15)]], 19: [nvm],
    }
    started, arrived = [], []

    def arrive(stage):
        arrived.append(stage)
        for ref in moved_by[stage]:
            wait_bytes(ref, recv.at[stage])

    def finish():
        for stage in dict.fromkeys(started):
            if stage not in arrived:
                arrive(stage)
            for ref in moved_by[stage]:
                wait_bytes(ref, send.at[stage])

    def dev(zc_to, g_to):
        return (zc_to % 2, (zc_to // 2) * 16 + (g_to % 4) * 4 + g_to // 4)

    def start(stage, src, dst, zc_to, g_to):
        started.append(stage)
        pltpu.make_async_remote_copy(
            src_ref=src, dst_ref=dst, send_sem=send.at[stage], recv_sem=recv.at[stage],
            device_id=dev(zc_to, g_to), device_id_type=MESH,
        ).start()

    def along_zc(stage, src, dst):
        @pl.loop(1, 16)
        def _(step):
            to = (zc + step) % 16
            start(stage, src.at[to], dst.at[zc], to, g)

    def along_g(stage, src, dst):
        @pl.loop(1, 16)
        def _(step):
            to = (g + step) % 16
            start(stage, src.at[to], dst.at[g], zc, to)

    barrier = pltpu.get_barrier_semaphore()

    @pl.loop(1, 16)
    def _(step):
        pl.semaphore_signal(barrier, 1, device_id=dev((zc + step) % 16, g), device_id_type=MESH)
        pl.semaphore_signal(barrier, 1, device_id=dev(zc, (g + step) % 16), device_id_type=MESH)

    half = pl.ds(pl.multiple_of(c * 512, 512), 512)
    copies = [
        pltpu.make_async_copy(src, dst, local.at[n])
        for n, (src, dst) in enumerate(
            ((ids_hbm, ids_ref), (x_hbm, x_ref), (prior_hbm, prior_ref), (cent_hbm.at[:, half], cvm), (rot_hbm, rvm))
        )
    ]
    for copy in copies:
        copy.start()
    copies[0].wait()

    ids = ids_ref[...]
    owner_row = ids >> 10
    eye = iota((128, 128), 0) == iota((128, 128), 1)
    owner_col = jnp.sum(jnp.where(eye, owner_row, 0), axis=1, keepdims=True)
    same = jnp.where(owner_col == owner_row, 1.0, 0.0)
    earlier = jnp.where(iota((128, 128), 0) < iota((128, 128), 1), same, 0.0)
    later = jnp.where(iota((128, 128), 1) < iota((128, 128), 0), same, 0.0)
    rank_row = jnp.sum(earlier, axis=0, keepdims=True)
    rank_col = jnp.sum(later, axis=1, keepdims=True)
    cold_owner_row = jnp.where(rank_row > 0.5, -1, owner_row)
    cold_owner_col = jnp.where(rank_col > 0.5, -1, owner_col)

    tile_row = iota((16, 128), 0)
    info = jnp.where(tile_row == 12, owner_row, 0)
    info = jnp.where(tile_row == 13, (ids & 1023) >> 5, info)
    info = jnp.where(tile_row == 14, ids & 31, info).astype(F32)
    info = jnp.where(tile_row == 15, rank_row, info)
    copies[1].wait()
    for cc in range(2):
        tile = info
        for j in range(4):
            match = (tile_row >= j * 3) & (tile_row < j * 3 + 3) & ((tile_row - (j * 3 - 1)).astype(F32) == rank_row)
            low = cc * 512 + j * 128
            tile = tile + mm(onehot(match), x_ref[:, low : low + 128])
        hbuf[cc] = tile.astype(BF)
    p0, p1 = iota((256, 256), 0), iota((256, 256), 1)
    perm[...] = onehot((p0 >> 4 == p1 & 15) & (p0 & 15 == p1 >> 4))

    def swap(rows):
        return mm(perm[...], rows).astype(BF)

    hr[zc] = hbuf[c]
    pl.semaphore_wait(barrier, 30)

    @pl.loop(1, 16)
    def _(step):
        to = (zc + step) % 16
        start(20, hbuf.at[to % 2], hr.at[zc], to, g)

    r256 = iota((256, 128), 0)
    hit = owner_at((r256 & 15) >> 1, r256 >> 4) == cold_owner_row
    rows_out = mm(onehot(hit & ((r256 & 1) == 0)), x_ref[:, 0:512])
    rows_out = rows_out + mm(onehot(hit & ((r256 & 1) == 1)), x_ref[:, 512:1024])
    bbuf[...] = rows_out.astype(BF).reshape(16, 16, 512)
    rb1[g] = bbuf[g]
    along_g(1, bbuf, rb1)

    copies[2].wait()
    ones = jnp.ones((128, 128), BF)
    for a in range(8):
        diag = jnp.where(eye, prior_ref[a : a + 1, :].astype(F32), 0.0).astype(BF)
        prior_of[a * 128 : a * 128 + 128, :] = mm(diag, ones).astype(BF)

    arrive(20)
    hot_rows = mm(perm[...], hr[...].reshape(256, 128))
    hot = hot_rows.astype(BF)
    for j, (ref, low) in enumerate(((hot_a, 0), (hot_a, 128), (hot_b, 0), (hot_b, 128))):
        ref[:, y, x, :, low : low + 128] = hot[j * 48 : j * 48 + 48].reshape(3, 16, 128)
    got = hot_rows[192:256].astype(I32)
    idb[g] = (got[48:64] << 17) + (got[0:16] << 10) + (got[16:32] << 5) + got[32:48]

    @pl.loop(1, 16)
    def _(step):
        start(8, idb.at[g], idb.at[g], zc, (g + step) % 16)

    for step in range(1, 4):
        to = y * 4 + (x + step) % 4
        start(4, hot_a.at[:, y, x], hot_a.at[:, y, x], zc, to)
        start(6, hot_b.at[:, y, x], hot_b.at[:, y, x], zc, ((y + step) % 4) * 4 + x)

    arrive(1)
    b2[...] = swap(rb1[...].reshape(256, 512)).reshape(16, 16, 512)
    rb2[zc] = b2[zc]
    along_zc(3, b2, rb2)

    arrive(4)
    arrive(6)
    for step in range(1, 4):
        to = ((y + step) % 4) * 4 + x
        start(5, hot_a.at[:, y], hot_a.at[:, y], zc, to)
        start(7, hot_b.at[:, :, x], hot_b.at[:, :, x], zc, y * 4 + (x + step) % 4)

    arrive(8)
    code = idb[...].reshape(256, 128)
    mine = ((code >> 10) & 127) == li
    rank = code >> 17
    number = (code & 1023) + 1
    ones8 = jnp.ones((8, 256), BF)
    ones256 = jnp.ones((256, 128), BF)
    lanes, rows = [], []
    for s in range(4):
        here = mine & (rank == s)
        top = jnp.where(here, number & 2016, 0).astype(F32).astype(BF)
        low = jnp.where(here, number & 31, 0).astype(F32).astype(BF)
        both = jnp.concatenate([top, low], axis=1)
        lane = lax.dot_general(ones8, both, (((1,), (1,)), ((), ())), preferred_element_type=F32)
        lane = lane.astype(I32)[0:1, :]
        lanes.append(jnp.where(lane == 0, -2, lane - 1))
        rows.append(mm(both, ones256).astype(I32) - 1)
    copies[3].wait()
    for s in range(4):
        block = slice(s * 256, s * 256 + 256)
        for a in range(8):
            wt[block, a * 128 : a * 128 + 128] = onehot(iota((256, 128), 1) + a * 128 == rows[s])
        for t in range(4):
            for h in range(2):
                low = t * 256 + h * 128
                mates[block, low : low + 128] = onehot(rows[s] == lanes[t][:, h * 128 : h * 128 + 128])
        crow[block, :] = mm(wt[block, :], cvm[...]).astype(BF)
        total = mm(mates[block, :], jnp.ones((1024, 128), BF))
        nrow[block, :] = total
        irow[block, :] = 1.0 / jnp.maximum(mm(wt[block, :], prior_of[...]) + total, 1.0)

    def twice(rows128):
        return jnp.concatenate([rows128] * 2, axis=1)

    def begin(part, cold_rows):
        cols = slice(part * 256, part * 256 + 256)
        for a in range(4):
            block = slice(a * 256, a * 256 + 256)
            acc[part, block, :] = mm(mates[block, 0:256], cold_rows) - twice(nrow[block, :]) * crow[block, cols].astype(F32)

    def near_rows(part, a, hot_rows):
        block = slice(a * 256, a * 256 + 256)
        change = acc[part, block, :] + mm(mates[block, 256:1024], hot_rows)
        return (crow[block, part * 256 : part * 256 + 256].astype(F32) + change * twice(irow[block, :])).astype(BF)

    arrive(3)
    cold[...] = swap(rb2[...].reshape(256, 512))
    begin(0, cold[:, 0:256])
    begin(1, cold[:, 256:512])

    arrive(5)
    for k in range(3):
        gha[k] = near_rows(0, k + 1, hot_a[...].reshape(768, 256)).reshape(4, 4, 16, 256)
    for step in range(1, 4):
        to = (y + step) % 4
        start(12, gha.at[:, to], rha.at[y], zc, to * 4 + x)
    arrive(7)
    for k in range(3):
        ghb[k] = near_rows(1, k + 1, hot_b[...].reshape(768, 256)).reshape(4, 4, 16, 256)
    for step in range(1, 4):
        to = (x + step) % 4
        start(13, ghb.at[:, :, to], rhb.at[x], zc, y * 4 + to)
    for part, hot_part in enumerate((hot_a, hot_b)):
        ready = swap(near_rows(part, 0, hot_part[...].reshape(768, 256)))
        gb[:, :, part * 256 : part * 256 + 256] = ready.reshape(16, 16, 256)
    rgb[zc] = gb[zc]
    along_zc(11, gb, rgb)
    rha[y] = gha[:, y]
    rhb[x] = ghb[:, :, x]

    for t in range(4):
        for a in range(8):
            w[a * 128 : a * 128 + 128, t * 256 : t * 256 + 256] = onehot(iota((128, 256), 0) + a * 128 == lanes[t])

    for a in range(4):
        lists = slice(a * 256, a * 256 + 256)
        count = mm(w[lists, :], jnp.ones((1024, 128), BF))
        scale = twice(1.0 / (prior_of[lists, :].astype(F32) + count))
        for part, hot_rows in enumerate((hot_a, hot_b)):
            cols = slice(part * 256, part * 256 + 256)
            old = cvm[lists, cols].astype(F32)
            sums = mm(w[lists, 0:256], cold[:, cols]) + mm(w[lists, 256:1024], hot_rows[...].reshape(768, 256))
            nvm[lists, cols] = (old + (sums - twice(count) * old) * scale).astype(BF)
    start(19, nvm, newc_hbm.at[:, half], zc + 1 - 2 * c, g)
    own_copy = pltpu.make_async_copy(nvm, newc_hbm.at[:, half], local.at[5])
    own_copy.start()

    arrive(12)
    h2a[...] = (rha[0] + rha[1]) + (rha[2] + rha[3])
    for step in range(1, 4):
        to = (x + step) % 4
        start(16, h2a.at[:, to], rh2a.at[x], zc, y * 4 + to)
    rh2a[x] = h2a[:, x]
    arrive(13)
    h2b[...] = (rhb[0] + rhb[1]) + (rhb[2] + rhb[3])
    for step in range(1, 4):
        to = (y + step) % 4
        start(17, h2b.at[:, to], rh2b.at[y], zc, to * 4 + x)
    rh2b[y] = h2b[:, y]

    arrive(11)
    fb[...] = swap(rgb[...].reshape(256, 512)).reshape(16, 16, 512)
    rfb[g] = fb[g]
    along_g(15, fb, rfb)

    arrive(16)
    arrive(17)
    back_a = ((rh2a[0] + rh2a[1]) + (rh2a[2] + rh2a[3])).reshape(48, 256)
    back_b = ((rh2b[0] + rh2b[1]) + (rh2b[2] + rh2b[3])).reshape(48, 256)
    back = jnp.concatenate(
        [back_a[:, :128], back_a[:, 128:], back_b[:, :128], back_b[:, 128:], jnp.zeros((64, 128), BF)], axis=0
    )
    ht[...] = swap(back).reshape(16, 16, 128)
    rht[zc] = ht[zc]
    along_zc(18, ht, rht)

    lane = iota((128, 256), 1)
    hit_col = owner_at((lane & 15) >> 1, lane >> 4) == cold_owner_col
    arrive(15)
    picked = [mm(onehot(hit_col & (lane & 1 == cc)), rfb[...].reshape(256, 512)) for cc in range(2)]
    arrive(18)
    tile_lane = iota((128, 16), 1)
    tiles = []
    for cc in range(2):
        tile = rht[cc]
        for zz in range(1, 8):
            tile = tile + rht[zz * 2 + cc]
        for j in range(4):
            match = (tile_lane >= j * 3) & (tile_lane < j * 3 + 3) & ((tile_lane - (j * 3 - 1)).astype(F32) == rank_col)
            tiles.append(mm(onehot(match), tile))
    near = jnp.concatenate(picked, axis=1) + jnp.concatenate(tiles, axis=1)
    residual = (x_ref[...].astype(F32) - near).astype(BF)
    copies[4].wait()
    for a in range(4):
        cols = slice(a * 256, a * 256 + 256)
        out_ref[:, cols] = mm(residual, rvm[:, cols]).astype(BF)

    own_copy.wait()
    finish()


def hand_over(newc_from, rotated_from, newc_to, rotated_to, newc_here, rotated_here, sem_in, sem_out):
    moves = [(rotated_from, rotated_here, rotated_to)]
    for n in range(8):
        rows = pl.ds(n * 128, 128)
        moves.append((newc_from.at[rows], newc_here.at[rows], newc_to.at[rows]))
    reads = [pltpu.make_async_copy(src, mid, sem_in.at[n]) for n, (src, mid, _) in enumerate(moves)]
    writes = [pltpu.make_async_copy(mid, dst, sem_out.at[n]) for n, (_, mid, dst) in enumerate(moves)]
    for read in reads:
        read.start()
    for read, write in zip(reads, writes):
        read.wait()
        write.start()
    for write in writes:
        write.wait()


def per_device(inserts, list_ids, centroids, prior_counts, rotation):
    square, tall, plane = (16, 16, 512), (3, 4, 4, 16, 256), (4, 3, 16, 256)
    shapes = [
        (2, 16, 128), (16, 16, 128), square, square, square, square, tall, tall,
        None, (1024, 1024), (1024, 1024), (1024, 1024), (1024, 512), (1024, 128), (256, 512), None, None, (1024, 512), (1024, 1024), (1024, 512), None,
        square, tall, tall, square, (4, 3, 4, 16, 256), (4, 3, 4, 16, 256), square, square,
        (3, 4, 16, 256), (3, 4, 16, 256), plane, plane, (16, 16, 128), (16, 16, 128), (256, 256),
    ]
    others = [
        pltpu.VMEM((16, 16, 128), I32),
        pltpu.VMEM((1024, 128), F32),
        pltpu.VMEM((1024, 128), F32),
        pltpu.VMEM((2, 1024, 256), F32),
    ]
    scratch = [pltpu.VMEM(shape, BF) if shape else others.pop(0) for shape in shapes]
    given = [pltpu.VMEM((1, 128), I32), pltpu.VMEM(inserts.shape, BF), pltpu.VMEM((8, 128), I32)]
    vmem = pl.BlockSpec(memory_space=pltpu.VMEM)
    anywhere = pl.BlockSpec(memory_space=pl.ANY)
    results = (jax.ShapeDtypeStruct(centroids.shape, BF), jax.ShapeDtypeStruct(inserts.shape, BF))
    made = pl.pallas_call(
        kernel,
        out_shape=results,
        in_specs=[pl.BlockSpec(memory_space=pltpu.HBM)] * 5,
        out_specs=(anywhere, vmem),
        scratch_shapes=given
        + scratch
        + [
            pltpu.SemaphoreType.DMA((STAGES,)),
            pltpu.SemaphoreType.DMA((STAGES,)),
            pltpu.SemaphoreType.DMA((6,)),
        ],
        compiler_params=pltpu.CompilerParams(
            collective_id=0, has_side_effects=True, vmem_limit_bytes=58 * 1024 * 1024
        ),
        cost_estimate=pl.CostEstimate(flops=4_000_000_000, bytes_accessed=8_000_000, transcendentals=0),
    )(list_ids.reshape(1, 128), inserts, prior_counts.reshape(8, 128), centroids, rotation)
    hbm = pl.BlockSpec(memory_space=pltpu.HBM)
    return pl.pallas_call(
        hand_over,
        out_shape=results,
        in_specs=[anywhere] * 2,
        out_specs=(hbm, hbm),
        scratch_shapes=[
            pltpu.VMEM(centroids.shape, BF),
            pltpu.VMEM(inserts.shape, BF),
            pltpu.SemaphoreType.DMA((9,)),
            pltpu.SemaphoreType.DMA((9,)),
        ],
    )(*made)


def solution(mesh):
    placed = (
        P(("replica", "lists"), None),
        P(("replica", "lists")),
        P("lists", None),
        P("lists"),
        P(),
    )
    return jax.shard_map(
        per_device,
        mesh=mesh,
        in_specs=placed,
        out_specs=(P("lists", None), P(("replica", "lists"), None)),
        check_vma=False,
    )
```

```python
import jax
import jax.numpy as jnp
from jax import lax
from jax.experimental import pallas as pl
from jax.experimental.pallas import tpu as pltpu
from jax.sharding import PartitionSpec as P

MESH = pl.DeviceIdType.MESH
BF = jnp.bfloat16
F32 = jnp.float32
I32 = jnp.int32
STAGES = 21


def mm(a, b):
    return jnp.dot(a, b, preferred_element_type=F32)


def iota(shape, dim):
    return lax.broadcasted_iota(I32, shape, dim)


def onehot(mask):
    return jnp.where(mask, 1.0, 0.0).astype(BF)


def owner_at(zz, gg):
    return (zz << 4) + ((gg & 3) << 2) + (gg >> 2)


def wait_bytes(ref, sem):
    pltpu.make_async_copy(ref, ref, sem).wait()


def kernel(
    ids_hbm, x_hbm, prior_hbm, cent_hbm, newc_hbm, rfb, rht,
    ids_ref, x_ref, prior_ref, hbuf, hr, bbuf, rb1, b2, rb2, hot_a, hot_b, idb,
    w, wt, mates, crow, prior_of, cold, nrow, irow, cvm, nvm, acc,
    gb, gha, ghb, rgb, rha, rhb, fb,
    h2a, h2b, rh2a, rh2b, ht, perm, send, recv, local,
):
    c = lax.axis_index("replica")
    li = lax.axis_index("lists")
    z = li // 16
    x = (li // 4) % 4
    y = li % 4
    zc = z * 2 + c
    g = y * 4 + x


    moved_by = {
        20: [hr.at[pl.ds(0, 15)]], 1: [bbuf.at[pl.ds(0, 15)]], 3: [b2.at[pl.ds(0, 15)]], 8: [idb.at[pl.ds(0, 15)]],
        4: [hot_a.at[:, 0, pl.ds(0, 3)]], 5: [hot_a.at[:, pl.ds(0, 3)]], 6: [hot_b.at[:, 0, pl.ds(0, 3)]],
        7: [hot_b.at[:, :, pl.ds(0, 3)]], 11: [gb.at[pl.ds(0, 15)]], 12: [gha.at[:, pl.ds(0, 3)]],
        13: [ghb.at[:, :, pl.ds(0, 3)]], 15: [fb.at[pl.ds(0, 15)]], 16: [h2a.at[:, pl.ds(0, 3)]],
        17: [h2b.at[:, pl.ds(0, 3)]], 18: [ht.at[pl.ds(0, 15)]], 19: [nvm],
    }
    started, arrived = [], []

    def arrive(stage):
        arrived.append(stage)
        for ref in moved_by[stage]:
            wait_bytes(ref, recv.at[stage])

    def finish():
        for stage in dict.fromkeys(started):
            if stage not in arrived:
                arrive(stage)
            for ref in moved_by[stage]:
                wait_bytes(ref, send.at[stage])

    def dev(zc_to, g_to):
        return (zc_to % 2, (zc_to // 2) * 16 + (g_to % 4) * 4 + g_to // 4)

    def start(stage, src, dst, zc_to, g_to):
        started.append(stage)
        pltpu.make_async_remote_copy(
            src_ref=src, dst_ref=dst, send_sem=send.at[stage], recv_sem=recv.at[stage],
            device_id=dev(zc_to, g_to), device_id_type=MESH,
        ).start()

    def along_zc(stage, src, dst):
        @pl.loop(1, 16)
        def _(step):
            to = (zc + step) % 16
            start(stage, src.at[to], dst.at[zc], to, g)

    def along_g(stage, src, dst):
        @pl.loop(1, 16)
        def _(step):
            to = (g + step) % 16
            start(stage, src.at[to], dst.at[g], zc, to)

    barrier = pltpu.get_barrier_semaphore()

    @pl.loop(1, 16)
    def _(step):
        pl.semaphore_signal(barrier, 1, device_id=dev((zc + step) % 16, g), device_id_type=MESH)
        pl.semaphore_signal(barrier, 1, device_id=dev(zc, (g + step) % 16), device_id_type=MESH)

    half = pl.ds(pl.multiple_of(c * 512, 512), 512)
    copies = [
        pltpu.make_async_copy(src, dst, local.at[n])
        for n, (src, dst) in enumerate(
            ((ids_hbm, ids_ref), (x_hbm, x_ref), (prior_hbm, prior_ref), (cent_hbm.at[:, half], cvm))
        )
    ]
    for copy in copies:
        copy.start()
    copies[0].wait()

    ids = ids_ref[...]
    owner_row = ids >> 10
    eye = iota((128, 128), 0) == iota((128, 128), 1)
    owner_col = jnp.sum(jnp.where(eye, owner_row, 0), axis=1, keepdims=True)
    same = jnp.where(owner_col == owner_row, 1.0, 0.0)
    earlier = jnp.where(iota((128, 128), 0) < iota((128, 128), 1), same, 0.0)
    rank_row = jnp.sum(earlier, axis=0, keepdims=True)
    cold_owner_row = jnp.where(rank_row > 0.5, -1, owner_row)

    tile_row = iota((16, 128), 0)
    info = jnp.where(tile_row == 12, owner_row, 0)
    info = jnp.where(tile_row == 13, (ids & 1023) >> 5, info)
    info = jnp.where(tile_row == 14, ids & 31, info).astype(F32)
    info = jnp.where(tile_row == 15, rank_row, info)
    copies[1].wait()
    for cc in range(2):
        tile = info
        for j in range(4):
            match = (tile_row >= j * 3) & (tile_row < j * 3 + 3) & ((tile_row - (j * 3 - 1)).astype(F32) == rank_row)
            low = cc * 512 + j * 128
            tile = tile + mm(onehot(match), x_ref[:, low : low + 128])
        hbuf[cc] = tile.astype(BF)
    p0, p1 = iota((256, 256), 0), iota((256, 256), 1)
    perm[...] = onehot((p0 >> 4 == p1 & 15) & (p0 & 15 == p1 >> 4))

    def swap(rows):
        return mm(perm[...], rows).astype(BF)

    r256 = iota((256, 128), 0)
    hit = owner_at((r256 & 15) >> 1, r256 >> 4) == cold_owner_row
    rows_out = mm(onehot(hit & ((r256 & 1) == 0)), x_ref[:, 0:512])
    rows_out = rows_out + mm(onehot(hit & ((r256 & 1) == 1)), x_ref[:, 512:1024])
    bbuf[...] = rows_out.astype(BF).reshape(16, 16, 512)
    rb1[g] = bbuf[g]
    hr[zc] = hbuf[c]
    pl.semaphore_wait(barrier, 30)

    @pl.loop(1, 16)
    def _(step):
        to = (zc + step) % 16
        start(20, hbuf.at[to % 2], hr.at[zc], to, g)

    along_g(1, bbuf, rb1)

    copies[2].wait()
    ones = jnp.ones((128, 128), BF)
    for a in range(8):
        diag = jnp.where(eye, prior_ref[a : a + 1, :].astype(F32), 0.0).astype(BF)
        prior_of[a * 128 : a * 128 + 128, :] = mm(diag, ones).astype(BF)

    arrive(20)
    hot_rows = mm(perm[...], hr[...].reshape(256, 128))
    hot = hot_rows.astype(BF)
    for j, (ref, low) in enumerate(((hot_a, 0), (hot_a, 128), (hot_b, 0), (hot_b, 128))):
        ref[:, y, x, :, low : low + 128] = hot[j * 48 : j * 48 + 48].reshape(3, 16, 128)
    for step in range(1, 4):
        to = y * 4 + (x + step) % 4
        start(4, hot_a.at[:, y, x], hot_a.at[:, y, x], zc, to)
        start(6, hot_b.at[:, y, x], hot_b.at[:, y, x], zc, ((y + step) % 4) * 4 + x)
    got = hot_rows[192:256].astype(I32)
    idb[g] = (got[48:64] << 17) + (got[0:16] << 10) + (got[16:32] << 5) + got[32:48]

    @pl.loop(1, 16)
    def _(step):
        start(8, idb.at[g], idb.at[g], zc, (g + step) % 16)

    arrive(1)
    b2[...] = swap(rb1[...].reshape(256, 512)).reshape(16, 16, 512)
    rb2[zc] = b2[zc]
    along_zc(3, b2, rb2)

    arrive(4)
    arrive(6)
    for step in range(1, 4):
        to = ((y + step) % 4) * 4 + x
        start(5, hot_a.at[:, y], hot_a.at[:, y], zc, to)
        start(7, hot_b.at[:, :, x], hot_b.at[:, :, x], zc, y * 4 + (x + step) % 4)

    arrive(8)
    code = idb[...].reshape(256, 128)
    mine = ((code >> 10) & 127) == li
    rank = code >> 17
    number = (code & 1023) + 1
    ones8 = jnp.ones((8, 256), BF)
    ones256 = jnp.ones((256, 128), BF)
    lanes, rows = [], []
    for s in range(4):
        here = mine & (rank == s)
        top = jnp.where(here, number & 2016, 0).astype(F32).astype(BF)
        low = jnp.where(here, number & 31, 0).astype(F32).astype(BF)
        both = jnp.concatenate([top, low], axis=1)
        lane = lax.dot_general(ones8, both, (((1,), (1,)), ((), ())), preferred_element_type=F32)
        lane = lane.astype(I32)[0:1, :]
        lanes.append(jnp.where(lane == 0, -2, lane - 1))
        rows.append(mm(both, ones256).astype(I32) - 1)
    copies[3].wait()
    for s in range(4):
        block = slice(s * 256, s * 256 + 256)
        for a in range(8):
            wt[block, a * 128 : a * 128 + 128] = onehot(iota((256, 128), 1) + a * 128 == rows[s])
        for t in range(4):
            for h in range(2):
                low = t * 256 + h * 128
                mates[block, low : low + 128] = onehot(rows[s] == lanes[t][:, h * 128 : h * 128 + 128])
        crow[block, :] = mm(wt[block, :], cvm[...]).astype(BF)
        total = mm(mates[block, :], jnp.ones((1024, 128), BF))
        nrow[block, :] = total
        irow[block, :] = 1.0 / jnp.maximum(mm(wt[block, :], prior_of[...]) + total, 1.0)

    def twice(rows128):
        return jnp.concatenate([rows128] * 2, axis=1)

    def begin(part, cold_rows):
        cols = slice(part * 256, part * 256 + 256)
        for a in range(4):
            block = slice(a * 256, a * 256 + 256)
            acc[part, block, :] = mm(mates[block, 0:256], cold_rows) - twice(nrow[block, :]) * crow[block, cols].astype(F32)

    def near_rows(part, a, hot_rows):
        block = slice(a * 256, a * 256 + 256)
        change = acc[part, block, :] + mm(mates[block, 256:1024], hot_rows)
        return (crow[block, part * 256 : part * 256 + 256].astype(F32) + change * twice(irow[block, :])).astype(BF)

    arrive(3)
    cold[...] = swap(rb2[...].reshape(256, 512))
    begin(0, cold[:, 0:256])
    begin(1, cold[:, 256:512])

    arrive(5)
    for k in range(3):
        gha[k] = near_rows(0, k + 1, hot_a[...].reshape(768, 256)).reshape(4, 4, 16, 256)
    for step in range(1, 4):
        to = (y + step) % 4
        start(12, gha.at[:, to], rha.at[y], zc, to * 4 + x)
    arrive(7)
    for k in range(3):
        ghb[k] = near_rows(1, k + 1, hot_b[...].reshape(768, 256)).reshape(4, 4, 16, 256)
    for step in range(1, 4):
        to = (x + step) % 4
        start(13, ghb.at[:, :, to], rhb.at[x], zc, y * 4 + to)
    for part, hot_part in enumerate((hot_a, hot_b)):
        ready = swap(near_rows(part, 0, hot_part[...].reshape(768, 256)))
        gb[:, :, part * 256 : part * 256 + 256] = ready.reshape(16, 16, 256)
    rgb[zc] = gb[zc]
    along_zc(11, gb, rgb)
    rha[y] = gha[:, y]
    rhb[x] = ghb[:, :, x]

    for t in range(4):
        for a in range(8):
            w[a * 128 : a * 128 + 128, t * 256 : t * 256 + 256] = onehot(iota((128, 256), 0) + a * 128 == lanes[t])

    for a in range(4):
        lists = slice(a * 256, a * 256 + 256)
        count = mm(w[lists, :], jnp.ones((1024, 128), BF))
        scale = twice(1.0 / (prior_of[lists, :].astype(F32) + count))
        for part, hot_rows in enumerate((hot_a, hot_b)):
            cols = slice(part * 256, part * 256 + 256)
            old = cvm[lists, cols].astype(F32)
            sums = mm(w[lists, 0:256], cold[:, cols]) + mm(w[lists, 256:1024], hot_rows[...].reshape(768, 256))
            nvm[lists, cols] = (old + (sums - twice(count) * old) * scale).astype(BF)
    start(19, nvm, newc_hbm.at[:, half], zc + 1 - 2 * c, g)
    own_copy = pltpu.make_async_copy(nvm, newc_hbm.at[:, half], local.at[5])
    own_copy.start()

    arrive(12)
    h2a[...] = (rha[0] + rha[1]) + (rha[2] + rha[3])
    for step in range(1, 4):
        to = (x + step) % 4
        start(16, h2a.at[:, to], rh2a.at[x], zc, y * 4 + to)
    rh2a[x] = h2a[:, x]
    arrive(13)
    h2b[...] = (rhb[0] + rhb[1]) + (rhb[2] + rhb[3])
    for step in range(1, 4):
        to = (y + step) % 4
        start(17, h2b.at[:, to], rh2b.at[y], zc, to * 4 + x)
    rh2b[y] = h2b[:, y]

    arrive(11)
    fb[...] = swap(rgb[...].reshape(256, 512)).reshape(16, 16, 512)
    own_fb = pltpu.make_async_copy(fb.at[g], rfb.at[g], local.at[4])
    own_fb.start()
    along_g(15, fb, rfb)

    arrive(16)
    arrive(17)
    back_a = ((rh2a[0] + rh2a[1]) + (rh2a[2] + rh2a[3])).reshape(48, 256)
    back_b = ((rh2b[0] + rh2b[1]) + (rh2b[2] + rh2b[3])).reshape(48, 256)
    back = jnp.concatenate(
        [back_a[:, :128], back_a[:, 128:], back_b[:, :128], back_b[:, 128:], jnp.zeros((64, 128), BF)], axis=0
    )
    ht[...] = swap(back).reshape(16, 16, 128)
    own_ht = pltpu.make_async_copy(ht.at[zc], rht.at[zc], local.at[6])
    own_ht.start()
    along_zc(18, ht, rht)

    own_fb.wait()
    own_ht.wait()
    own_copy.wait()
    finish()


def finish_rows(
    ids_hbm, x_hbm, rot_hbm, newc_from, rfb_from, rht_from, newc_to, rotated_to,
    ids_ref, x_ref, rvm, newc_here, rfb, rht, rotated, sem_in, sem_out,
):
    given = ((ids_hbm, ids_ref), (rfb_from, rfb), (rht_from, rht), (x_hbm, x_ref), (rot_hbm, rvm))
    reads = [pltpu.make_async_copy(src, dst, sem_in.at[n]) for n, (src, dst) in enumerate(given)]
    for read in reads:
        read.start()
    halves = [pl.ds(n * 256, 256) for n in range(4)]
    table_in = [pltpu.make_async_copy(newc_from.at[rows], newc_here.at[rows], sem_in.at[5 + n]) for n, rows in enumerate(halves)]
    table_out = [pltpu.make_async_copy(newc_here.at[rows], newc_to.at[rows], sem_out.at[n]) for n, rows in enumerate(halves)]
    for copy in table_in:
        copy.start()

    reads[0].wait()
    owner_row = ids_ref[...] >> 10
    eye = iota((128, 128), 0) == iota((128, 128), 1)
    owner_col = jnp.sum(jnp.where(eye, owner_row, 0), axis=1, keepdims=True)
    same = jnp.where(owner_col == owner_row, 1.0, 0.0)
    later = jnp.where(iota((128, 128), 1) < iota((128, 128), 0), same, 0.0)
    rank_col = jnp.sum(later, axis=1, keepdims=True)
    lane = iota((128, 256), 1)
    hit_col = owner_at((lane & 15) >> 1, lane >> 4) == jnp.where(rank_col > 0.5, -1, owner_col)
    reads[1].wait()
    picked = [mm(onehot(hit_col & (lane & 1 == cc)), rfb[...].reshape(256, 512)) for cc in range(2)]
    reads[2].wait()
    tile_lane = iota((128, 16), 1)
    tiles = []
    for cc in range(2):
        tile = rht[cc]
        for zz in range(1, 8):
            tile = tile + rht[zz * 2 + cc]
        for j in range(4):
            match = (tile_lane >= j * 3) & (tile_lane < j * 3 + 3) & ((tile_lane - (j * 3 - 1)).astype(F32) == rank_col)
            tiles.append(mm(onehot(match), tile))
    near = jnp.concatenate(picked, axis=1) + jnp.concatenate(tiles, axis=1)
    reads[3].wait()
    residual = (x_ref[...].astype(F32) - near).astype(BF)
    reads[4].wait()
    for copy_in, copy_out in zip(table_in, table_out):
        copy_in.wait()
        copy_out.start()
    sent = []
    for a in range(4):
        cols = slice(a * 256, a * 256 + 256)
        rotated[:, cols] = mm(residual, rvm[:, cols]).astype(BF)
        sent.append(pltpu.make_async_copy(rotated.at[:, pl.ds(a * 256, 256)], rotated_to.at[:, pl.ds(a * 256, 256)], sem_out.at[4 + a]))
        sent[a].start()
    for copy in table_out + sent:
        copy.wait()


def per_device(inserts, list_ids, centroids, prior_counts, rotation):
    square, tall, plane = (16, 16, 512), (3, 4, 4, 16, 256), (4, 3, 16, 256)
    shapes = [
        (2, 16, 128), (16, 16, 128), square, square, square, square, tall, tall,
        None, (1024, 1024), (1024, 1024), (1024, 1024), (1024, 512), (1024, 128), (256, 512), None, None, (1024, 512), (1024, 512), None,
        square, tall, tall, square, (4, 3, 4, 16, 256), (4, 3, 4, 16, 256), square,
        (3, 4, 16, 256), (3, 4, 16, 256), plane, plane, (16, 16, 128), (256, 256),
    ]
    others = [
        pltpu.VMEM((16, 16, 128), I32),
        pltpu.VMEM((1024, 128), F32),
        pltpu.VMEM((1024, 128), F32),
        pltpu.VMEM((2, 1024, 256), F32),
    ]
    scratch = [pltpu.VMEM(shape, BF) if shape else others.pop(0) for shape in shapes]
    given = [pltpu.VMEM((1, 128), I32), pltpu.VMEM(inserts.shape, BF), pltpu.VMEM((8, 128), I32)]
    anywhere, hbm = pl.BlockSpec(memory_space=pl.ANY), pl.BlockSpec(memory_space=pltpu.HBM)
    ids = list_ids.reshape(1, 128)
    back_rows, back_tiles = jax.ShapeDtypeStruct(square, BF), jax.ShapeDtypeStruct((16, 16, 128), BF)
    table, rows_of = jax.ShapeDtypeStruct(centroids.shape, BF), jax.ShapeDtypeStruct(inserts.shape, BF)
    made = pl.pallas_call(
        kernel,
        out_shape=(table, back_rows, back_tiles),
        in_specs=[hbm] * 4,
        out_specs=(anywhere,) * 3,
        scratch_shapes=given
        + scratch
        + [
            pltpu.SemaphoreType.DMA((STAGES,)),
            pltpu.SemaphoreType.DMA((STAGES,)),
            pltpu.SemaphoreType.DMA((7,)),
        ],
        compiler_params=pltpu.CompilerParams(
            collective_id=0, has_side_effects=True, vmem_limit_bytes=58 * 1024 * 1024
        ),
        cost_estimate=pl.CostEstimate(flops=4_000_000_000, bytes_accessed=8_000_000, transcendentals=0),
    )(ids, inserts, prior_counts.reshape(8, 128), centroids)
    return pl.pallas_call(
        finish_rows,
        out_shape=(table, rows_of),
        in_specs=[anywhere] * 6,
        out_specs=(hbm, hbm),
        scratch_shapes=[
            pltpu.VMEM((1, 128), I32),
            pltpu.VMEM(inserts.shape, BF),
            pltpu.VMEM(rotation.shape, BF),
            pltpu.VMEM(centroids.shape, BF),
            pltpu.VMEM(square, BF),
            pltpu.VMEM((16, 16, 128), BF),
            pltpu.VMEM(inserts.shape, BF),
            pltpu.SemaphoreType.DMA((9,)),
            pltpu.SemaphoreType.DMA((8,)),
        ],
        compiler_params=pltpu.CompilerParams(vmem_limit_bytes=58 * 1024 * 1024),
        cost_estimate=pl.CostEstimate(flops=400_000_000, bytes_accessed=9_000_000, transcendentals=0),
    )(ids, inserts, rotation, *made)


def solution(mesh):
    placed = (
        P(("replica", "lists"), None),
        P(("replica", "lists")),
        P("lists", None),
        P("lists"),
        P(),
    )
    return jax.shard_map(
        per_device,
        mesh=mesh,
        in_specs=placed,
        out_specs=(P("lists", None), P(("replica", "lists"), None)),
        check_vma=False,
    )
```

```python
import jax
import jax.numpy as jnp
from jax import lax
from jax.experimental import pallas as pl
from jax.experimental.pallas import tpu as pltpu
from jax.sharding import PartitionSpec as P

MESH = pl.DeviceIdType.MESH
BF = jnp.bfloat16
F32 = jnp.float32
I32 = jnp.int32
STAGES = 25


def mm(a, b):
    return jnp.dot(a, b, preferred_element_type=F32)


def iota(shape, dim):
    return lax.broadcasted_iota(I32, shape, dim)


def onehot(mask):
    return jnp.where(mask, 1.0, 0.0).astype(BF)


def owner_at(zz, gg):
    return (zz << 4) + ((gg & 3) << 2) + (gg >> 2)


def wait_bytes(ref, sem):
    pltpu.make_async_copy(ref, ref, sem).wait()


def kernel(
    ids_hbm, x_hbm, prior_hbm, cent_hbm, newc_hbm, rfb, rht,
    ids_ref, x_ref, prior_ref, hbuf, hr, bbuf, rb1, b2, rb2, hot_a, hot_b, idb,
    w, wt, mates, crow, prior_of, cold, nrow, irow, cvm, nvm, acc,
    gb, gha, ghb, rgb, rha, rhb, fb,
    h2a, h2b, rh2a, rh2b, ht, perm, send, recv, local,
):
    c = lax.axis_index("replica")
    li = lax.axis_index("lists")
    z = li // 16
    x = (li // 4) % 4
    y = li % 4
    zc = z * 2 + c
    g = y * 4 + x


    moved_by = {
        20: [hr.at[pl.ds(0, 15)]], 1: [bbuf.at[pl.ds(0, 15)]], 3: [b2.at[pl.ds(0, 15)]], 8: [idb.at[pl.ds(0, 15)]],
        4: [hot_a.at[:, 0, pl.ds(0, 3)]], 5: [hot_a.at[:, pl.ds(0, 3), pl.ds(0, 3)]], 6: [hot_b.at[:, 0, pl.ds(0, 3)]],
        7: [hot_b.at[:, pl.ds(0, 3), pl.ds(0, 3)]], 21: [hot_a.at[:, 0, pl.ds(0, 3)]], 22: [hot_b.at[:, 0, pl.ds(0, 3)]], 11: [gb.at[pl.ds(0, 15)]], 12: [gha.at[:, pl.ds(0, 3), pl.ds(0, 3)]], 23: [gha.at[:, 0, pl.ds(0, 3)]],
        13: [ghb.at[:, pl.ds(0, 3), pl.ds(0, 3)]], 24: [ghb.at[:, 0, pl.ds(0, 3)]], 15: [fb.at[pl.ds(0, 15)]], 16: [h2a.at[:, pl.ds(0, 3)]],
        17: [h2b.at[:, pl.ds(0, 3)]], 18: [ht.at[pl.ds(0, 15)]], 19: [nvm],
    }
    started, arrived = [], []

    def arrive(stage):
        arrived.append(stage)
        for ref in moved_by[stage]:
            wait_bytes(ref, recv.at[stage])

    def finish():
        for stage in dict.fromkeys(started):
            if stage not in arrived:
                arrive(stage)
            for ref in moved_by[stage]:
                wait_bytes(ref, send.at[stage])

    def dev(zc_to, g_to):
        return (zc_to % 2, (zc_to // 2) * 16 + (g_to % 4) * 4 + g_to // 4)

    def start(stage, src, dst, zc_to, g_to):
        started.append(stage)
        pltpu.make_async_remote_copy(
            src_ref=src, dst_ref=dst, send_sem=send.at[stage], recv_sem=recv.at[stage],
            device_id=dev(zc_to, g_to), device_id_type=MESH,
        ).start()

    def along_zc(stage, src, dst):
        @pl.loop(1, 16)
        def _(step):
            to = (zc + step) % 16
            start(stage, src.at[to], dst.at[zc], to, g)

    def along_g(stage, src, dst):
        @pl.loop(1, 16)
        def _(step):
            to = (g + step) % 16
            start(stage, src.at[to], dst.at[g], zc, to)

    barrier = pltpu.get_barrier_semaphore()

    @pl.loop(1, 16)
    def _(step):
        pl.semaphore_signal(barrier, 1, device_id=dev((zc + step) % 16, g), device_id_type=MESH)
        pl.semaphore_signal(barrier, 1, device_id=dev(zc, (g + step) % 16), device_id_type=MESH)

    half = pl.ds(pl.multiple_of(c * 512, 512), 512)
    copies = [
        pltpu.make_async_copy(src, dst, local.at[n])
        for n, (src, dst) in enumerate(
            ((ids_hbm, ids_ref), (x_hbm, x_ref), (prior_hbm, prior_ref), (cent_hbm.at[:, half], cvm))
        )
    ]
    for copy in copies:
        copy.start()
    copies[0].wait()

    ids = ids_ref[...]
    owner_row = ids >> 10
    eye = iota((128, 128), 0) == iota((128, 128), 1)
    owner_col = jnp.sum(jnp.where(eye, owner_row, 0), axis=1, keepdims=True)
    same = jnp.where(owner_col == owner_row, 1.0, 0.0)
    earlier = jnp.where(iota((128, 128), 0) < iota((128, 128), 1), same, 0.0)
    rank_row = jnp.sum(earlier, axis=0, keepdims=True)
    cold_owner_row = jnp.where(rank_row > 0.5, -1, owner_row)

    tile_row = iota((16, 128), 0)
    info = jnp.where(tile_row == 12, owner_row, 0)
    info = jnp.where(tile_row == 13, (ids & 1023) >> 5, info)
    info = jnp.where(tile_row == 14, ids & 31, info).astype(F32)
    info = jnp.where(tile_row == 15, rank_row, info)
    copies[1].wait()
    for cc in range(2):
        tile = info
        for j in range(4):
            match = (tile_row >= j * 3) & (tile_row < j * 3 + 3) & ((tile_row - (j * 3 - 1)).astype(F32) == rank_row)
            low = cc * 512 + j * 128
            tile = tile + mm(onehot(match), x_ref[:, low : low + 128])
        hbuf[cc] = tile.astype(BF)
    p0, p1 = iota((256, 256), 0), iota((256, 256), 1)
    perm[...] = onehot((p0 >> 4 == p1 & 15) & (p0 & 15 == p1 >> 4))

    def swap(rows):
        return mm(perm[...], rows).astype(BF)

    r256 = iota((256, 128), 0)
    hit = owner_at((r256 & 15) >> 1, r256 >> 4) == cold_owner_row
    rows_out = mm(onehot(hit & ((r256 & 1) == 0)), x_ref[:, 0:512])
    rows_out = rows_out + mm(onehot(hit & ((r256 & 1) == 1)), x_ref[:, 512:1024])
    bbuf[...] = rows_out.astype(BF).reshape(16, 16, 512)
    rb1[g] = bbuf[g]
    hr[zc] = hbuf[c]
    pl.semaphore_wait(barrier, 30)

    @pl.loop(1, 16)
    def _(step):
        to = (zc + step) % 16
        start(20, hbuf.at[to % 2], hr.at[zc], to, g)

    along_g(1, bbuf, rb1)

    copies[2].wait()
    ones = jnp.ones((128, 128), BF)
    for a in range(8):
        diag = jnp.where(eye, prior_ref[a : a + 1, :].astype(F32), 0.0).astype(BF)
        prior_of[a * 128 : a * 128 + 128, :] = mm(diag, ones).astype(BF)

    arrive(20)
    hot_rows = mm(perm[...], hr[...].reshape(256, 128))
    hot = hot_rows.astype(BF)
    for j, (ref, low) in enumerate(((hot_a, 0), (hot_a, 128), (hot_b, 0), (hot_b, 128))):
        ref[:, y, x, :, low : low + 128] = hot[j * 48 : j * 48 + 48].reshape(3, 16, 128)
    for step in range(1, 4):
        to = y * 4 + (x + step) % 4
        start(4, hot_a.at[:, y, x], hot_a.at[:, y, x], zc, to)
        start(6, hot_b.at[:, y, x], hot_b.at[:, y, x], zc, ((y + step) % 4) * 4 + x)
    for step in range(1, 4):
        start(21, hot_a.at[:, y, x], hot_a.at[:, y, x], zc, ((y + step) % 4) * 4 + x)
        start(22, hot_b.at[:, y, x], hot_b.at[:, y, x], zc, y * 4 + (x + step) % 4)
    got = hot_rows[192:256].astype(I32)
    idb[g] = (got[48:64] << 17) + (got[0:16] << 10) + (got[16:32] << 5) + got[32:48]

    @pl.loop(1, 16)
    def _(step):
        start(8, idb.at[g], idb.at[g], zc, (g + step) % 16)

    arrive(1)
    b2[...] = swap(rb1[...].reshape(256, 512)).reshape(16, 16, 512)
    rb2[zc] = b2[zc]
    along_zc(3, b2, rb2)

    arrive(4)
    arrive(6)
    for step in range(1, 4):
        to = ((y + step) % 4) * 4 + x
        for other in range(1, 4):
            xx, yy = (x + other) % 4, (y + other) % 4
            start(5, hot_a.at[:, y, xx], hot_a.at[:, y, xx], zc, to)
            start(7, hot_b.at[:, yy, x], hot_b.at[:, yy, x], zc, y * 4 + (x + step) % 4)

    arrive(8)
    code = idb[...].reshape(256, 128)
    mine = ((code >> 10) & 127) == li
    rank = code >> 17
    number = (code & 1023) + 1
    ones8 = jnp.ones((8, 256), BF)
    ones256 = jnp.ones((256, 128), BF)
    lanes, rows = [], []
    for s in range(4):
        here = mine & (rank == s)
        top = jnp.where(here, number & 2016, 0).astype(F32).astype(BF)
        low = jnp.where(here, number & 31, 0).astype(F32).astype(BF)
        both = jnp.concatenate([top, low], axis=1)
        lane = lax.dot_general(ones8, both, (((1,), (1,)), ((), ())), preferred_element_type=F32)
        lane = lane.astype(I32)[0:1, :]
        lanes.append(jnp.where(lane == 0, -2, lane - 1))
        rows.append(mm(both, ones256).astype(I32) - 1)
    copies[3].wait()
    for s in range(4):
        block = slice(s * 256, s * 256 + 256)
        for a in range(8):
            wt[block, a * 128 : a * 128 + 128] = onehot(iota((256, 128), 1) + a * 128 == rows[s])
        for t in range(4):
            for h in range(2):
                low = t * 256 + h * 128
                mates[block, low : low + 128] = onehot(rows[s] == lanes[t][:, h * 128 : h * 128 + 128])
        crow[block, :] = mm(wt[block, :], cvm[...]).astype(BF)
        total = mm(mates[block, :], jnp.ones((1024, 128), BF))
        nrow[block, :] = total
        irow[block, :] = 1.0 / jnp.maximum(mm(wt[block, :], prior_of[...]) + total, 1.0)

    def twice(rows128):
        return jnp.concatenate([rows128] * 2, axis=1)

    def begin(part, cold_rows):
        cols = slice(part * 256, part * 256 + 256)
        for a in range(4):
            block = slice(a * 256, a * 256 + 256)
            acc[part, block, :] = mm(mates[block, 0:256], cold_rows) - twice(nrow[block, :]) * crow[block, cols].astype(F32)

    def near_rows(part, a, hot_rows):
        block = slice(a * 256, a * 256 + 256)
        change = acc[part, block, :] + mm(mates[block, 256:1024], hot_rows)
        return (crow[block, part * 256 : part * 256 + 256].astype(F32) + change * twice(irow[block, :])).astype(BF)

    arrive(3)
    cold[...] = swap(rb2[...].reshape(256, 512))
    begin(0, cold[:, 0:256])
    begin(1, cold[:, 256:512])

    arrive(5)
    arrive(21)
    for k in range(3):
        gha[k] = near_rows(0, k + 1, hot_a[...].reshape(768, 256)).reshape(4, 4, 16, 256)
    for step in range(1, 4):
        to = (y + step) % 4
        for other in range(1, 4):
            xx = (x + other) % 4
            start(12, gha.at[:, to, xx], rha.at[y, :, xx], zc, to * 4 + x)
    arrive(7)
    arrive(22)
    for k in range(3):
        ghb[k] = near_rows(1, k + 1, hot_b[...].reshape(768, 256)).reshape(4, 4, 16, 256)
    for step in range(1, 4):
        to = (x + step) % 4
        for other in range(1, 4):
            yy = (y + other) % 4
            start(13, ghb.at[:, yy, to], rhb.at[x, :, yy], zc, y * 4 + to)
    for step in range(1, 4):
        start(23, gha.at[:, (y + step) % 4, x], rha.at[y, :, x], zc, ((y + step) % 4) * 4 + x)
        start(24, ghb.at[:, y, (x + step) % 4], rhb.at[x, :, y], zc, y * 4 + (x + step) % 4)
    for part, hot_part in enumerate((hot_a, hot_b)):
        ready = swap(near_rows(part, 0, hot_part[...].reshape(768, 256)))
        gb[:, :, part * 256 : part * 256 + 256] = ready.reshape(16, 16, 256)
    rgb[zc] = gb[zc]
    along_zc(11, gb, rgb)
    rha[y] = gha[:, y]
    rhb[x] = ghb[:, :, x]

    for t in range(4):
        for a in range(8):
            w[a * 128 : a * 128 + 128, t * 256 : t * 256 + 256] = onehot(iota((128, 256), 0) + a * 128 == lanes[t])

    for a in range(4):
        lists = slice(a * 256, a * 256 + 256)
        count = mm(w[lists, :], jnp.ones((1024, 128), BF))
        scale = twice(1.0 / (prior_of[lists, :].astype(F32) + count))
        for part, hot_rows in enumerate((hot_a, hot_b)):
            cols = slice(part * 256, part * 256 + 256)
            old = cvm[lists, cols].astype(F32)
            sums = mm(w[lists, 0:256], cold[:, cols]) + mm(w[lists, 256:1024], hot_rows[...].reshape(768, 256))
            nvm[lists, cols] = (old + (sums - twice(count) * old) * scale).astype(BF)
    start(19, nvm, newc_hbm.at[:, half], zc + 1 - 2 * c, g)
    own_copy = pltpu.make_async_copy(nvm, newc_hbm.at[:, half], local.at[5])
    own_copy.start()

    def gathered(ref, at):
        return (ref[0, :, at] + ref[1, :, at]) + (ref[2, :, at] + ref[3, :, at])

    arrive(12)
    for step in range(1, 4):
        to = (x + step) % 4
        h2a[:, to] = gathered(rha, to)
        start(16, h2a.at[:, to], rh2a.at[x], zc, y * 4 + to)
    arrive(13)
    for step in range(1, 4):
        to = (y + step) % 4
        h2b[:, to] = gathered(rhb, to)
        start(17, h2b.at[:, to], rh2b.at[y], zc, to * 4 + x)
    arrive(23)
    rh2a[x] = gathered(rha, x)
    arrive(24)
    rh2b[y] = gathered(rhb, y)

    arrive(11)
    fb[...] = swap(rgb[...].reshape(256, 512)).reshape(16, 16, 512)
    own_fb = pltpu.make_async_copy(fb.at[g], rfb.at[g], local.at[4])
    own_fb.start()
    along_g(15, fb, rfb)

    arrive(16)
    arrive(17)
    back_a = ((rh2a[0] + rh2a[1]) + (rh2a[2] + rh2a[3])).reshape(48, 256)
    back_b = ((rh2b[0] + rh2b[1]) + (rh2b[2] + rh2b[3])).reshape(48, 256)
    back = jnp.concatenate(
        [back_a[:, :128], back_a[:, 128:], back_b[:, :128], back_b[:, 128:], jnp.zeros((64, 128), BF)], axis=0
    )
    ht[...] = swap(back).reshape(16, 16, 128)
    own_ht = pltpu.make_async_copy(ht.at[zc], rht.at[zc], local.at[6])
    own_ht.start()
    along_zc(18, ht, rht)

    own_fb.wait()
    own_ht.wait()
    own_copy.wait()
    finish()


def finish_rows(
    ids_hbm, x_hbm, rot_hbm, newc_from, rfb_from, rht_from, newc_to, rotated_to,
    ids_ref, x_ref, rvm, newc_here, rfb, rht, rotated, sem_in, sem_out,
):
    given = ((ids_hbm, ids_ref), (rfb_from, rfb), (rht_from, rht), (x_hbm, x_ref), (rot_hbm, rvm))
    reads = [pltpu.make_async_copy(src, dst, sem_in.at[n]) for n, (src, dst) in enumerate(given)]
    for read in reads:
        read.start()
    halves = [pl.ds(n * 256, 256) for n in range(4)]
    table_in = [pltpu.make_async_copy(newc_from.at[rows], newc_here.at[rows], sem_in.at[5 + n]) for n, rows in enumerate(halves)]
    table_out = [pltpu.make_async_copy(newc_here.at[rows], newc_to.at[rows], sem_out.at[n]) for n, rows in enumerate(halves)]
    for copy in table_in:
        copy.start()

    reads[0].wait()
    owner_row = ids_ref[...] >> 10
    eye = iota((128, 128), 0) == iota((128, 128), 1)
    owner_col = jnp.sum(jnp.where(eye, owner_row, 0), axis=1, keepdims=True)
    same = jnp.where(owner_col == owner_row, 1.0, 0.0)
    later = jnp.where(iota((128, 128), 1) < iota((128, 128), 0), same, 0.0)
    rank_col = jnp.sum(later, axis=1, keepdims=True)
    lane = iota((128, 256), 1)
    hit_col = owner_at((lane & 15) >> 1, lane >> 4) == jnp.where(rank_col > 0.5, -1, owner_col)
    reads[1].wait()
    picked = [mm(onehot(hit_col & (lane & 1 == cc)), rfb[...].reshape(256, 512)) for cc in range(2)]
    reads[2].wait()
    tile_lane = iota((128, 16), 1)
    tiles = []
    for cc in range(2):
        tile = rht[cc]
        for zz in range(1, 8):
            tile = tile + rht[zz * 2 + cc]
        for j in range(4):
            match = (tile_lane >= j * 3) & (tile_lane < j * 3 + 3) & ((tile_lane - (j * 3 - 1)).astype(F32) == rank_col)
            tiles.append(mm(onehot(match), tile))
    near = jnp.concatenate(picked, axis=1) + jnp.concatenate(tiles, axis=1)
    reads[3].wait()
    residual = (x_ref[...].astype(F32) - near).astype(BF)
    reads[4].wait()
    for copy_in, copy_out in zip(table_in, table_out):
        copy_in.wait()
        copy_out.start()
    sent = []
    for a in range(4):
        cols = slice(a * 256, a * 256 + 256)
        rotated[:, cols] = mm(residual, rvm[:, cols]).astype(BF)
        sent.append(pltpu.make_async_copy(rotated.at[:, pl.ds(a * 256, 256)], rotated_to.at[:, pl.ds(a * 256, 256)], sem_out.at[4 + a]))
        sent[a].start()
    for copy in table_out + sent:
        copy.wait()


def per_device(inserts, list_ids, centroids, prior_counts, rotation):
    square, tall, plane = (16, 16, 512), (3, 4, 4, 16, 256), (4, 3, 16, 256)
    shapes = [
        (2, 16, 128), (16, 16, 128), square, square, square, square, tall, tall,
        None, (1024, 1024), (1024, 1024), (1024, 1024), (1024, 512), (1024, 128), (256, 512), None, None, (1024, 512), (1024, 512), None,
        square, tall, tall, square, (4, 3, 4, 16, 256), (4, 3, 4, 16, 256), square,
        (3, 4, 16, 256), (3, 4, 16, 256), plane, plane, (16, 16, 128), (256, 256),
    ]
    others = [
        pltpu.VMEM((16, 16, 128), I32),
        pltpu.VMEM((1024, 128), F32),
        pltpu.VMEM((1024, 128), F32),
        pltpu.VMEM((2, 1024, 256), F32),
    ]
    scratch = [pltpu.VMEM(shape, BF) if shape else others.pop(0) for shape in shapes]
    given = [pltpu.VMEM((1, 128), I32), pltpu.VMEM(inserts.shape, BF), pltpu.VMEM((8, 128), I32)]
    anywhere, hbm = pl.BlockSpec(memory_space=pl.ANY), pl.BlockSpec(memory_space=pltpu.HBM)
    ids = list_ids.reshape(1, 128)
    back_rows, back_tiles = jax.ShapeDtypeStruct(square, BF), jax.ShapeDtypeStruct((16, 16, 128), BF)
    table, rows_of = jax.ShapeDtypeStruct(centroids.shape, BF), jax.ShapeDtypeStruct(inserts.shape, BF)
    made = pl.pallas_call(
        kernel,
        out_shape=(table, back_rows, back_tiles),
        in_specs=[hbm] * 4,
        out_specs=(anywhere,) * 3,
        scratch_shapes=given
        + scratch
        + [
            pltpu.SemaphoreType.DMA((STAGES,)),
            pltpu.SemaphoreType.DMA((STAGES,)),
            pltpu.SemaphoreType.DMA((7,)),
        ],
        compiler_params=pltpu.CompilerParams(
            collective_id=0, has_side_effects=True, vmem_limit_bytes=58 * 1024 * 1024
        ),
        cost_estimate=pl.CostEstimate(flops=4_000_000_000, bytes_accessed=8_000_000, transcendentals=0),
    )(ids, inserts, prior_counts.reshape(8, 128), centroids)
    return pl.pallas_call(
        finish_rows,
        out_shape=(table, rows_of),
        in_specs=[anywhere] * 6,
        out_specs=(hbm, hbm),
        scratch_shapes=[
            pltpu.VMEM((1, 128), I32),
            pltpu.VMEM(inserts.shape, BF),
            pltpu.VMEM(rotation.shape, BF),
            pltpu.VMEM(centroids.shape, BF),
            pltpu.VMEM(square, BF),
            pltpu.VMEM((16, 16, 128), BF),
            pltpu.VMEM(inserts.shape, BF),
            pltpu.SemaphoreType.DMA((9,)),
            pltpu.SemaphoreType.DMA((8,)),
        ],
        compiler_params=pltpu.CompilerParams(vmem_limit_bytes=58 * 1024 * 1024),
        cost_estimate=pl.CostEstimate(flops=400_000_000, bytes_accessed=9_000_000, transcendentals=0),
    )(ids, inserts, rotation, *made)


def solution(mesh):
    placed = (
        P(("replica", "lists"), None),
        P(("replica", "lists")),
        P("lists", None),
        P("lists"),
        P(),
    )
    return jax.shard_map(
        per_device,
        mesh=mesh,
        in_specs=placed,
        out_specs=(P("lists", None), P(("replica", "lists"), None)),
        check_vma=False,
    )
```
